32 devices in a mesh: runs: 2 (over x), gy: 16 (over z, y, core).
Axes of the slice: x: 2, y: 2, z: 4, core: 2. Of those that a mesh axis runs over, the one named last changes fastest.
Arguments:
- depth: float32 [1024, 1920], P(('runs', 'gy')), parts along dimension 0, may hold values from 0.02 to 3
- flux_east: float32 [1024, 1920], P(('runs', 'gy')), parts along dimension 0, may hold values from -2 to 2
- flux_south: float32 [1024, 1920], P(('runs', 'gy')), parts along dimension 0, may hold values from -2 to 2
- river_section: float32 [4096], P(('runs', 'gy')), parts along dimension 0, may hold values from 0 to 2
- bed_level: float32 [512, 1920], P('gy'), may hold values from -3 to 3
- rough_class: int32 [512, 1920], P('gy'), may hold values from 0 to 7
- manning_table: float32 [8], replicated, may hold values from 0.02 to 0.15
- bank_cell: int32 [4, 2048], P(None, 'gy'), may hold values from 0 to 983039, as said below
Outputs:
- depth_out: float32 [1024, 1920], P(('runs', 'gy')), parts along dimension 0
- east_out: float32 [1024, 1920], P(('runs', 'gy')), parts along dimension 0
- south_out: float32 [1024, 1920], P(('runs', 'gy')), parts along dimension 0
- section_out: float32 [4096], P(('runs', 'gy')), parts along dimension 0
The draws below stay inside these ranges and needn't reach their ends.
There are 2 independent parts, one for each index of `runs`. The reference program is written for one: setup_inputs(seed, part) draws one part's arguments, and reference() takes and returns one part's arrays. A program takes and returns all parts, laid end to end along the dimension named above; an argument that names none is the same for every part. Nothing has to cross between parts.
Inputs may be any that keep to these rules, and one draw needn't show every extreme that they name: `bank_cell`: the 4 corridor cells of a node are consecutive flat indices row * 1920 + column within one map row. Node n is owned by gy index o = n // 128, and all its corridor cells lie in map rows from max((o - 1) * 32, 0) to min((o + 2) * 32, 512) - 1.
All inputs are finite; a program needn't handle non-finite values.
Results may differ from the reference program's by a relative error of at most 0.00013.
Values sent between devices are 32-bit elements; how exact they have to be, the bound alone decides.
A program may use at most 64 MiB of HBM per device.

```python
import math
import jax
import jax.numpy as jnp

RY = 32
NX = 1920
NODE_DEV = 128
K = 4
CLASSES = 8
STEPS = 4
NY = 512
NODES = 2048


def draw_bank_cell(key, part):
    tiles = NODES // NODE_DEV
    key_start, key_walk, key_jitter = jax.random.split(key, 3)
    node = jnp.arange(NODES, dtype=jnp.int32)
    owner = node // NODE_DEV
    place = node % NODE_DEV
    jitter = jax.random.randint(key_jitter, (NODES,), 0, 2).astype(jnp.int32)
    row = (owner - 1) * RY + place * 3 * RY // NODE_DEV + jitter
    row = jnp.clip(row, jnp.maximum((owner - 1) * RY, 0), jnp.minimum((owner + 2) * RY - 1, NY - 1))
    start = jax.random.randint(key_start, (tiles, 1), 0, NX - K + 1).astype(jnp.int32)
    moves = jax.random.randint(key_walk, (tiles, NODE_DEV), -2, 3).astype(jnp.int32)
    column = jnp.clip(start + jnp.cumsum(moves, axis=1), 0, NX - K).reshape(-1).astype(jnp.int32)
    row = row.at[0].set(0).at[NODES - 1].set(NY - 1)
    column = column.at[0].set(0).at[NODES - 1].set(NX - K)
    flat = row * NX + column
    return (flat[None, :] + jnp.arange(K, dtype=jnp.int32)[:, None]).astype(jnp.int32)


def plant(result, rng, low, top_value):
    dims = result.shape
    index_at = [jax.random.randint(jax.random.fold_in(rng, axis), (), 0, dims[axis]) for axis in range(len(dims))]
    result = result.at[tuple(index_at)].set(low)
    longest = dims.index(max(dims))
    index_at[longest] = (index_at[longest] + 1) % dims[longest]
    return result.at[tuple(index_at)].set(top_value)


def shard_levels(stream_key, dims, cuts, low, largest):
    def one(position, blocks):
        heights = jax.random.uniform(jax.random.fold_in(jax.random.fold_in(stream_key, 6), position), (blocks,), jnp.float32, low / len(cuts), largest / len(cuts))
        return jnp.repeat(jnp.exp(heights), dims[position] // blocks).reshape((-1,) + (1,) * (len(dims) - position - 1))

    factor_of = one(*cuts[0])
    for cut in cuts[1:]:
        factor_of = factor_of * one(*cut)
    return factor_of


def noise(rng, shape, scale, reach, cuts=(), held_as=jnp.bfloat16):
    level = shard_levels(rng, shape, cuts, -0.22, 0.18) if cuts else 1.0
    result = jax.random.normal(rng, shape, jnp.float32) * scale * level
    return jnp.minimum(jnp.maximum(result, -reach), reach).astype(held_as)


def setup_inputs(seed: int = 0, part: int = 0) -> dict:
    key_of = jax.random.split(jax.random.key(seed), 9)
    part_splits = jax.random.split(jax.random.fold_in(key_of[8], part), 9)
    return {
        "depth": jnp.clip(jnp.exp(math.log(3.0) - 5.0106353 * jax.random.uniform(part_splits[0], (NY, NX), jnp.float32) ** shard_levels(part_splits[0], (NY, NX), ((0, 16),), -0.2, 0.2)), 0.02, 3.0),
        "flux_east": noise(part_splits[1], (NY, NX), 0.3, 2.0, ((0, 16),), jnp.float32),
        "flux_south": noise(part_splits[2], (NY, NX), 0.3, 2.0, ((0, 16),), jnp.float32),
        "river_section": jnp.clip(2.0 * jax.random.uniform(part_splits[3], (NODES,), jnp.float32) ** shard_levels(part_splits[3], (NODES,), ((0, 16),), -0.2, 0.2), 0.0, 2.0),
        "bed_level": noise(key_of[4], (NY, NX), 0.5, 3.0, ((0, 16),), jnp.float32),
        "rough_class": plant(jax.random.randint(key_of[5], (NY, NX), 0, CLASSES), jax.random.fold_in(key_of[5], 1), 0, CLASSES - 1).astype(jnp.int32),
        "manning_table": jnp.clip(jnp.exp(jax.random.uniform(key_of[6], (CLASSES,), jnp.float32, math.log(0.02), math.log(0.15))), 0.02, 0.15),
        "bank_cell": draw_bank_cell(jax.random.fold_in(key_of[8], 71), part),
    }


GRAV = 9.81
TSTEP = 8.0
CELL = 90.0
FLOOR = 0.05
BANK_COEF = 200.0
CELL_AREA = 8100.0
NODE_AREA = 20000.0


def face_flux(flux, surf_a, surf_b, bed_a, bed_b, mann_a, mann_b):
    flow_depth = jnp.maximum(jnp.maximum(surf_a, surf_b) - jnp.maximum(bed_a, bed_b), FLOOR)
    mean_mann = 0.5 * (mann_a + mann_b)
    driven = flux - GRAV * flow_depth * TSTEP * (surf_b - surf_a) / CELL
    damping = 1.0 + GRAV * TSTEP * mean_mann * mean_mann * jnp.abs(flux) / jnp.power(flow_depth, 7.0 / 3.0)
    return driven / damping


def reference(depth, flux_east, flux_south, river_section, bed_level, rough_class, manning_table, bank_cell):
    manning = manning_table[rough_class]
    rows_all, cols_all = depth.shape
    for substep in range(STEPS):
        surface = depth + bed_level
        east_part = face_flux(flux_east[:, :-1], surface[:, :-1], surface[:, 1:], bed_level[:, :-1], bed_level[:, 1:], manning[:, :-1], manning[:, 1:])
        flux_east = jnp.concatenate([east_part, jnp.zeros((rows_all, 1), jnp.float32)], axis=1)
        south_part = face_flux(flux_south[:-1], surface[:-1], surface[1:], bed_level[:-1], bed_level[1:], manning[:-1], manning[1:])
        flux_south = jnp.concatenate([south_part, jnp.zeros((1, cols_all), jnp.float32)], axis=0)
        surf_flat = surface.reshape(-1)
        bank_flow = BANK_COEF * (river_section[None, :] - surf_flat[bank_cell])
        source = jnp.zeros((rows_all * cols_all,), jnp.float32).at[bank_cell.reshape(-1)].add(bank_flow.reshape(-1)).reshape(rows_all, cols_all)
        east_in = jnp.concatenate([jnp.zeros((rows_all, 1), jnp.float32), flux_east[:, :-1]], axis=1)
        south_in = jnp.concatenate([jnp.zeros((1, cols_all), jnp.float32), flux_south[:-1]], axis=0)
        depth = depth + TSTEP / CELL * (east_in - flux_east + south_in - flux_south) + TSTEP * source / CELL_AREA
        river_section = river_section - TSTEP * jnp.sum(bank_flow, axis=0) / NODE_AREA
    return depth, flux_east, flux_south, river_section
```

```python
import math

import jax
import jax.numpy as jnp
from jax import lax
from jax.experimental import pallas as pl
from jax.experimental.pallas import tpu as pltpu
from jax.sharding import PartitionSpec as P

STEPS = 4
HALO = STEPS
LANES = 128
TILE = 8

GRAV = 9.81
TSTEP = 8.0
CELL = 90.0
FLOOR = 0.05
BANK_COEF = 200.0
CELL_AREA = 8100.0
NODE_AREA = 20000.0

SLOPE = GRAV * TSTEP / CELL
LEVEL = SLOPE * TSTEP / CELL
FLOW = LEVEL * TSTEP / CELL
ROUGH = math.sqrt(0.25 * GRAV * TSTEP * LEVEL ** (7.0 / 3.0) / FLOW)
KEEP = 1.0 - TSTEP * BANK_COEF * 4.0 / NODE_AREA
GAIN = TSTEP * BANK_COEF / NODE_AREA
INTO = TSTEP * BANK_COEF / CELL_AREA

MESH = pl.DeviceIdType.MESH
VMEM_BYTES = 24 * 1024 * 1024
FAR = -(1 << 24)
OFFSETS = (-1, 1, -2, 2)


def wave(batches):
    running, waiting = [], list(batches)
    while running or waiting:
        if waiting:
            running.extend(waiting.pop(0))
        for unit in list(running):
            try:
                next(unit)
            except StopIteration:
                running.remove(unit)


def by(size, units):
    units = list(units)
    return [units[i : i + size] for i in range(0, len(units), size)]


def halves(value):
    high = value.astype(jnp.bfloat16)
    return high, (value - high.astype(jnp.float32)).astype(jnp.bfloat16)


def flood_kernel(
    table_in,
    depth_in,
    east_in,
    south_in,
    bed_in,
    rough_in,
    section_in,
    cells_in,
    depth_out,
    east_out,
    south_out,
    section_out,
    table,
    raw,
    raw_rough,
    edge,
    edge_rough,
    surf,
    fe,
    fs,
    bed,
    mann,
    max_e,
    max_s,
    drag_e,
    drag_s,
    tally,
    number,
    number4,
    boxes,
    partial,
    sections,
    cells,
    part,
    low,
    high,
    in_sem,
    strip_ssem,
    strip_rsem,
    node_ssem,
    node_rsem,
    part_ssem,
    part_rsem,
):
    me = lax.axis_index("gy")
    tiles = lax.axis_size("gy")
    rows, columns = depth_in.shape
    ext = rows + 2 * HALO
    chunks = columns // LANES
    owned = section_in.shape[1]
    total = 5 * owned

    def there(offset):
        return (me + offset >= 0) & (me + offset < tiles)

    def absent(offset):
        return jnp.logical_not(there(offset))

    barrier = pltpu.get_barrier_semaphore()
    for offset in OFFSETS:
        @pl.when(there(offset))
        def _():
            pl.semaphore_signal(
                barrier, inc=1, device_id={"gy": me + offset}, device_id_type=MESH
            )

    fields = (depth_in, bed_in, east_in, south_in)
    loads = [
        pltpu.make_async_copy(source, target, in_sem.at[i])
        for i, (source, target) in enumerate(
            [(field, raw.at[i]) for i, field in enumerate(fields)]
            + [
                (rough_in, raw_rough),
                (table_in, table),
                (section_in, sections.at[2]),
                (cells_in, cells.at[2]),
            ]
        )
    ]
    for load in loads:
        load.start()

    def send(src, dst, ssem, rsem, offset):
        return pltpu.make_async_remote_copy(
            src_ref=src,
            dst_ref=dst,
            send_sem=ssem,
            recv_sem=rsem,
            device_id={"gy": me + offset},
            device_id_type=MESH,
        )

    node_sends = {}
    for i, offset in enumerate(OFFSETS):
        slot = 2 - offset
        node_sends[offset] = (
            send(section_in, sections.at[slot], node_ssem.at[0, i], node_rsem.at[0, i], offset),
            send(cells_in, cells.at[slot], node_ssem.at[1, i], node_rsem.at[1, i], offset),
        )
    strip_sends = {}
    for i, offset in enumerate((-1, 1)):
        theirs = slice(0, HALO) if offset < 0 else slice(rows - HALO, rows)
        lands = slice(0, HALO) if offset < 0 else slice(HALO, 2 * HALO)
        sources = [field.at[theirs] for field in fields] + [rough_in.at[theirs]]
        targets = [edge.at[j, lands] for j in range(4)] + [edge_rough.at[lands]]
        strip_sends[offset] = [
            send(source, target, strip_ssem.at[i, j], strip_rsem.at[i, j], offset)
            for j, (source, target) in enumerate(zip(sources, targets))
        ]

    pl.semaphore_wait(barrier, jnp.minimum(me, 2) + jnp.minimum(tiles - 1 - me, 2))
    for offset in OFFSETS:
        @pl.when(there(offset))
        def _():
            for copy in node_sends[offset]:
                copy.start()

    for offset in (-1, 1):
        @pl.when(there(offset))
        def _():
            for copy in strip_sends[offset]:
                copy.start()

    for load in loads:
        load.wait()

    scaled = [table[k] * ROUGH for k in range(table.shape[0])]

    def roughness(rough):
        values, bit = scaled, 1
        while len(values) > 1:
            odd = (rough & bit) != 0
            values = [
                jnp.where(odd, values[i + 1], values[i]) if i + 1 < len(values) else values[i]
                for i in range(0, len(values), 2)
            ]
            bit *= 2
        return values[0]

    def at(c):
        return slice(LANES * c, LANES * (c + 1))

    lane_id = lax.broadcasted_iota(jnp.int32, (1, LANES), 1)

    def turn(value, shift):
        return pltpu.roll(value, LANES - shift, 1)

    def lanes_to(value, preceding, shift):
        mixed = jnp.where(lane_id >= LANES - shift, preceding, value)
        return pltpu.roll(mixed, shift, 1)

    def south(value):
        return pltpu.roll(value, value.shape[0] - 1, 0)

    def north(value):
        return pltpu.roll(value, 1, 0)

    row_id = lax.broadcasted_iota(jnp.int32, (TILE, LANES), 0)
    shut_last = (row_id == TILE - 1) & (me == tiles - 1)
    shut_first = (row_id == TILE - 1) & (me == 0)

    def depth_of(surf_a, surf_b, bed_top):
        return jnp.maximum(jnp.maximum(surf_a, surf_b) - bed_top, FLOOR * LEVEL)

    def power_log(flow_depth):
        return jnp.log(flow_depth) * (-7.0 / 3.0)

    def damping(flux, drag, power):
        return 1.0 / (1.0 + drag * jnp.abs(flux) * power)

    def square(value):
        return value * value

    def closed_east(c, flux):
        return jnp.where(lane_id == LANES - 1, 0.0, flux) if c == chunks - 1 else flux

    def closed_south(flux):
        count = flux.shape[0]
        return jnp.concatenate(
            [flux[: count - 2 * TILE]] * (count > 2 * TILE)
            + [
                jnp.where(shut_last, 0.0, flux[count - 2 * TILE : count - TILE]),
                jnp.where(shut_first, 0.0, flux[count - TILE :]),
            ],
            axis=0,
        )

    def last_four(value, carried):
        pair = value + lanes_to(value, carried[0], 1)
        return pair + lanes_to(pair, carried[1], 2), (value, pair)

    def zeros(count):
        return jnp.zeros((count, LANES), jnp.float32)

    after = {}

    def put(name, c, value):
        after[name, c] = value

    def got(name, c, count):
        return after.get((name, c), zeros(count))

    inner = rows - TILE

    def own_chunk(c):
        floor = raw[1, :, at(c)] * LEVEL
        bed[:rows, at(c)] = floor
        mine = roughness(raw_rough[:, at(c)])
        mann[:rows, at(c)] = mine
        here = raw[0, :, at(c)] * LEVEL + floor
        surf[:rows, at(c)] = here
        turned = [turn(a, 1) for a in (here, floor, mine)]
        put("own", c, (here, turned))
        yield
        yield
        following = after.get(("own", c + 1), (zeros(rows), [zeros(rows)] * 3))
        east, floor_e, mann_e = (
            jnp.where(lane_id < LANES - 1, a, b) for a, b in zip(turned, following[1])
        )
        pair = here + east
        pair_next = following[0] + following[1][0]
        mixed = turn(jnp.where(lane_id < 2, pair_next, pair), 2)
        top = jnp.maximum(floor, floor_e)
        drag = square(mine + mann_e)
        max_e[:rows, at(c)] = top
        drag_e[:rows, at(c)] = drag
        depth_e = depth_of(here, east, top)
        log_e = power_log(depth_e)
        below_s = south(here)[:inner]
        top = jnp.maximum(floor, south(floor))[:inner]
        drag_b = square((mine + south(mine))[:inner])
        max_s[:inner, at(c)] = top
        drag_s[:inner, at(c)] = drag_b
        depth_s = depth_of(here[:inner], below_s, top)
        log_s = power_log(depth_s)
        yield
        boxes[:rows, at(c)] = pair + mixed
        power_e, power_s = jnp.exp(log_e), jnp.exp(log_s)
        flux_e = raw[2, :, at(c)] * FLOW
        flux_s = raw[3, :inner, at(c)] * FLOW
        yield
        damp_e = damping(flux_e, drag, power_e)
        damp_s = damping(flux_s, drag_b, power_s)
        yield
        new_east = closed_east(c, (flux_e - depth_e * (east - here)) * damp_e)
        new_south = (flux_s - depth_s * (below_s - here[:inner])) * damp_s
        fe[:rows, at(c)] = new_east
        fs[:inner, at(c)] = new_south
        put("east", c, new_east)
        west = lanes_to(new_east, got("east", c - 1, rows), 1)
        yield
        partial[:, at(c)] = here + (west - new_east)

    wave(by(1, (own_chunk(c) for c in range(chunks))))
    after.clear()

    for offset in OFFSETS:
        @pl.when(there(-offset))
        def _():
            for copy in node_sends[offset]:
                copy.wait_recv()

        @pl.when(absent(-offset))
        def _():
            sections[2 - offset] = jnp.zeros((1, owned), jnp.float32)
            cells[2 - offset] = jnp.full((cells.shape[1], owned), FAR, jnp.int32)

    section = jnp.concatenate([sections[i] for i in range(5)], axis=1)
    cell = jnp.concatenate([cells[i, 0:1, :] for i in range(5)], axis=1)
    local = cell - (me * rows - HALO) * columns
    valid = (local >= 0) & (local < ext * columns)
    local = jnp.where(valid, local, 0)
    from_top = ((local.astype(jnp.float32) + 0.5) * (1.0 / columns)).astype(jnp.int32)
    column = local - from_top * columns
    chunk = column >> 7
    lane = column & (LANES - 1)
    own = valid & (from_top >= HALO) & (from_top < rows + HALO)
    place = jnp.where(own, chunk * rows + from_top - HALO, -1)
    near = slice(owned, 4 * owned)
    beyond = jnp.where(from_top < HALO, from_top + HALO, from_top - rows - HALO)
    place_edge = jnp.where(valid & jnp.logical_not(own), chunk * TILE + beyond, -1)

    def one_hot(count, index):
        hit = lax.broadcasted_iota(jnp.int32, (count, index.shape[1]), 0) == index
        return jnp.where(hit, 1.0, 0.0).astype(jnp.bfloat16)

    hit = one_hot(chunks * rows, place[:, near])
    hit_edge = one_hot(-(-chunks * TILE // 16) * 16, place_edge)
    lane_hit = lax.broadcasted_iota(jnp.int32, (LANES, total), 0) == lane
    levels = section * (LEVEL * INTO)
    level_high = levels.astype(jnp.bfloat16).astype(jnp.float32)
    weights = jnp.concatenate(
        [
            jnp.where(lane_hit, value, 0.0)
            for value in (level_high, levels - level_high, jnp.ones_like(levels))
        ],
        axis=0,
    ).astype(jnp.bfloat16)
    contract = (((1,), (1,)), ((), ()))
    spread = lax.dot_general(
        hit, weights[:, near], contract, preferred_element_type=jnp.float32
    )
    spread_edge = lax.dot_general(
        hit_edge, weights, contract, preferred_element_type=jnp.float32
    )
    summed = counted = (zeros(ext),) * 2
    for c in range(chunks):
        block = jnp.concatenate(
            [
                spread[c * rows : (c + 1) * rows],
                spread_edge[c * TILE : (c + 1) * TILE],
            ],
            axis=0,
        )
        level = block[:, :LANES] + block[:, LANES : 2 * LANES]
        tally[:, at(c)], summed = last_four(level, summed)
        count = block[:, 2 * LANES :] * INTO
        number4[:, at(c)], counted = last_four(count, counted)
        number[:, at(c)] = count * GAIN

    for i, offset in enumerate((-1, 1)):
        @pl.when(there(-offset))
        def _():
            for copy in strip_sends[offset]:
                copy.wait_recv()

        @pl.when(absent(-offset))
        def _():
            lands = slice(HALO * i, HALO * (i + 1))
            edge[:, lands, :] = jnp.zeros((4, HALO, columns), jnp.float32)
            edge_rough[lands, :] = jnp.zeros((HALO, columns), jnp.int32)

    outer = slice(rows, ext)

    def edge_chunk(c):
        floor = edge[1, :, at(c)] * LEVEL
        here = edge[0, :, at(c)] * LEVEL + floor
        mine = roughness(edge_rough[:, at(c)])
        turned = [turn(a, 1) for a in (here, floor, mine)]
        put("edge", c, (here, turned))
        yield
        yield
        following = after.get(("edge", c + 1), (zeros(TILE), [zeros(TILE)] * 3))
        east, floor_e, mann_e = (
            jnp.where(lane_id < LANES - 1, a, b) for a, b in zip(turned, following[1])
        )
        pair = here + east
        pair_next = following[0] + following[1][0]
        mixed = turn(jnp.where(lane_id < 2, pair_next, pair), 2)
        top = jnp.maximum(floor, floor_e)
        drag = square(mine + mann_e)
        max_e[outer, at(c)] = top
        drag_e[outer, at(c)] = drag
        depth_e = depth_of(here, east, top)
        log_e = power_log(depth_e)
        whole = jnp.concatenate([surf[:rows, at(c)], here], axis=0)
        below_s = south(whole)[inner:]
        floor = jnp.concatenate([bed[:rows, at(c)], floor], axis=0)
        mine = jnp.concatenate([mann[:rows, at(c)], mine], axis=0)
        top = jnp.maximum(floor, south(floor))[inner:]
        drag_b = square((mine + south(mine))[inner:])
        max_s[inner:, at(c)] = top
        drag_s[inner:, at(c)] = drag_b
        depth_s = depth_of(whole[inner:], below_s, top)
        log_s = power_log(depth_s)
        yield
        boxes[outer, at(c)] = pair + mixed
        power_e, power_s = jnp.exp(log_e), jnp.exp(log_s)
        flux_e = edge[2, :, at(c)] * FLOW
        flux_s = jnp.concatenate([raw[3, inner:, at(c)], edge[3, :, at(c)]], axis=0) * FLOW
        yield
        damp_e = damping(flux_e, drag, power_e)
        damp_s = damping(flux_s, drag_b, power_s)
        yield
        new_east = closed_east(c, (flux_e - depth_e * (east - here)) * damp_e)
        new_south = closed_south((flux_s - depth_s * (below_s - whole[inner:])) * damp_s)
        fe[outer, at(c)] = new_east
        fs[inner:, at(c)] = new_south
        put("edge_east", c, new_east)
        west = lanes_to(new_east, got("edge_east", c - 1, TILE), 1)
        new_south = jnp.concatenate([fs[:inner, at(c)], new_south], axis=0)
        yield
        surf[:, at(c)] = (
            jnp.concatenate([partial[:, at(c)], here + (west - new_east)], axis=0)
            + (north(new_south) - new_south)
            + (tally[:, at(c)] - number4[:, at(c)] * whole)
        )

    def chunk_step(step, c):
        last = step == STEPS - 1
        count = rows if last else ext
        span = slice(0, count)
        whole = surf[:, at(c)]
        here = whole[:count]
        turned = turn(here, 1)
        put(("here", step), c, (here, turned))
        yield
        yield
        following = after.get((("here", step), c + 1), (zeros(count), zeros(count)))
        east = jnp.where(lane_id < LANES - 1, turned, following[1])
        depth_e = depth_of(here, east, max_e[span, at(c)])
        log_e = power_log(depth_e)
        below_s = south(whole)
        depth_s = depth_of(whole, below_s, max_s[:, at(c)])
        log_s = power_log(depth_s)
        if not last:
            pair = here + east
            pair_next = following[0] + following[1]
            mixed = turn(jnp.where(lane_id < 2, pair_next, pair), 2)
        box = boxes[span, at(c)]
        moved = number[span, at(c)] * box
        put(("moved", step), c, moved)
        spill = lanes_to(moved, got(("moved", step), c - 1, count), 1)
        yield
        power_e, power_s = jnp.exp(log_e), jnp.exp(log_s)
        if not last:
            boxes[:, at(c)] = KEEP * box + (pair + mixed)
        spill = moved + spill
        put(("spill", step), c, spill)
        spill2 = lanes_to(spill, got(("spill", step), c - 1, count), 2)
        yield
        flux_e, flux_s = fe[span, at(c)], fs[:, at(c)]
        damp_e = damping(flux_e, drag_e[span, at(c)], power_e)
        damp_s = damping(flux_s, drag_s[:, at(c)], power_s)
        source = KEEP**step * tally[span, at(c)] + (spill + spill2) - number4[span, at(c)] * here
        yield
        new_east = closed_east(c, (flux_e - depth_e * (east - here)) * damp_e)
        new_south = closed_south((flux_s - depth_s * (below_s - whole)) * damp_s)
        put(("east", step), c, new_east)
        west = lanes_to(new_east, got(("east", step), c - 1, count), 1)
        if last:
            east_out[:, at(c)] = new_east * (1.0 / FLOW)
            south_out[:, at(c)] = new_south[:rows] * (1.0 / FLOW)
        else:
            fe[:, at(c)] = new_east
            fs[:, at(c)] = new_south
        yield
        level = here + (west - new_east) + (north(new_south) - new_south)[:count] + source
        if last:
            depth_out[:, at(c)] = level * (1.0 / LEVEL) - raw[1, :, at(c)]
        else:
            surf[:, at(c)] = level

    flat = {}

    def node_chunk(c):
        here = surf[:rows, at(c)]
        turned = turn(here, 1)
        put("node", c, (here, turned))
        yield
        yield
        following = after.get(("node", c + 1), (zeros(rows), zeros(rows)))
        pair = here + jnp.where(lane_id < LANES - 1, turned, following[1])
        pair_next = following[0] + following[1]
        mixed = turn(jnp.where(lane_id < 2, pair_next, pair), 2)
        yield
        flat[c] = KEEP * boxes[:rows, at(c)] + (pair + mixed)

    batches = by(3, (edge_chunk(c) for c in range(chunks))) + [[]]
    for step in range(1, STEPS - 1):
        batches += by(1, (chunk_step(step, c) for c in range(chunks)))
    wave(batches + [[]] * 5 + by(3, (node_chunk(c) for c in range(chunks))))
    flat = [flat[c] for c in range(chunks)]

    turned = jnp.concatenate(halves(jnp.concatenate(flat, axis=0).T), axis=0)
    picked = jnp.dot(turned, hit, preferred_element_type=jnp.float32)
    picked = picked[:LANES] + picked[LANES:]
    picked = jnp.sum(jnp.where(lane_hit[:, near], picked, 0.0), axis=0, keepdims=True)
    final = jnp.where(
        own[:, near], KEEP**STEPS * section[:, near] + (GAIN / LEVEL) * picked, 0.0
    )
    for i in range(3):
        part[i] = final[:, i * owned : (i + 1) * owned]

    part_prev = send(part.at[0], high, part_ssem.at[0], part_rsem.at[0], -1)
    part_next = send(part.at[2], low, part_ssem.at[1], part_rsem.at[1], 1)

    @pl.when(there(-1))
    def _():
        part_prev.start()

    @pl.when(there(1))
    def _():
        part_next.start()

    wave(by(1, (chunk_step(STEPS - 1, c) for c in range(chunks))))

    for offset in OFFSETS:
        @pl.when(there(offset))
        def _():
            for copy in node_sends[offset]:
                copy.wait_send()

    for offset in (-1, 1):
        @pl.when(there(offset))
        def _():
            for copy in strip_sends[offset]:
                copy.wait_send()

    section_out[...] = part[1]

    @pl.when(there(1))
    def _():
        part_prev.wait_recv()
        section_out[...] += high[...]

    @pl.when(there(-1))
    def _():
        part_next.wait_recv()
        section_out[...] += low[...]

    @pl.when(there(-1))
    def _():
        part_prev.wait_send()

    @pl.when(there(1))
    def _():
        part_next.wait_send()


def finish_kernel(a, b, c, d, a_out, b_out, c_out, d_out, out_sem):
    stores = [
        pltpu.make_async_copy(source, target, out_sem.at[i])
        for i, (source, target) in enumerate(
            ((a, a_out), (b, b_out), (c, c_out), (d, d_out))
        )
    ]
    for store in stores:
        store.start()
    for store in stores:
        store.wait()


def finish(*arrays):
    return pl.pallas_call(
        finish_kernel,
        out_shape=[jax.ShapeDtypeStruct(a.shape, a.dtype) for a in arrays],
        in_specs=[pl.BlockSpec(memory_space=pltpu.VMEM)] * 4,
        out_specs=[pl.BlockSpec(memory_space=pltpu.MemorySpace.HBM)] * 4,
        scratch_shapes=[pltpu.SemaphoreType.DMA((4,))],
        compiler_params=pltpu.CompilerParams(vmem_limit_bytes=VMEM_BYTES),
        name="finish",
    )(*arrays)


def local(
    depth, flux_east, flux_south, river_section, bed_level, rough_class, manning_table, bank_cell
):
    rows, columns = depth.shape
    owned = river_section.shape[0]
    width, _ = bank_cell.shape
    ext = rows + 2 * HALO
    operands = [
        pltpu.with_memory_space_constraint(a, pltpu.MemorySpace.HBM)
        for a in (
            manning_table,
            depth,
            flux_east,
            flux_south,
            bed_level,
            rough_class,
            river_section.reshape(1, owned),
            bank_cell,
        )
    ]
    hbm = pl.BlockSpec(memory_space=pltpu.MemorySpace.HBM)
    vmem = pl.BlockSpec(memory_space=pltpu.VMEM)
    tile = pltpu.VMEM((rows, columns), jnp.float32)
    line = pltpu.VMEM((1, owned), jnp.float32)
    wide = pltpu.VMEM((ext, columns), jnp.float32)
    dma = pltpu.SemaphoreType.DMA
    depth, flux_east, flux_south, section = pl.pallas_call(
        flood_kernel,
        out_shape=[tile, tile, tile, line],
        in_specs=[hbm] * 8,
        out_specs=[vmem] * 4,
        scratch_shapes=[
            pltpu.SMEM(manning_table.shape, jnp.float32),
            pltpu.VMEM((4, rows, columns), jnp.float32),
            pltpu.VMEM((rows, columns), jnp.int32),
            pltpu.VMEM((4, 2 * HALO, columns), jnp.float32),
            pltpu.VMEM((2 * HALO, columns), jnp.int32),
        ]
        + [wide] * 13
        + [
            tile,
            pltpu.VMEM((5, 1, owned), jnp.float32),
            pltpu.VMEM((5, width, owned), jnp.int32),
            pltpu.VMEM((3, 1, owned), jnp.float32),
            line,
            line,
            dma((8,)),
            dma((2, 5)),
            dma((2, 5)),
            dma((2, 4)),
            dma((2, 4)),
            dma((2,)),
            dma((2,)),
        ],
        compiler_params=pltpu.CompilerParams(
            collective_id=0, has_side_effects=True, vmem_limit_bytes=VMEM_BYTES
        ),
        name="flood",
    )(*operands)
    depth, flux_east, flux_south, section = finish(depth, flux_east, flux_south, section)
    return depth, flux_east, flux_south, section.reshape(owned)


def solution(mesh):
    return jax.shard_map(
        local,
        mesh=mesh,
        in_specs=(
            P(("runs", "gy"), None),
            P(("runs", "gy"), None),
            P(("runs", "gy"), None),
            P(("runs", "gy")),
            P("gy", None),
            P("gy", None),
            P(),
            P(None, "gy"),
        ),
        out_specs=(
            P(("runs", "gy"), None),
            P(("runs", "gy"), None),
            P(("runs", "gy"), None),
            P(("runs", "gy")),
        ),
        check_vma=False,
    )
```

```python
import math

import jax
import jax.numpy as jnp
from jax import lax
from jax.experimental import pallas as pl
from jax.experimental.pallas import tpu as pltpu
from jax.sharding import PartitionSpec as P

STEPS = 4
HALO = STEPS
SOON = HALO - 1
LANES = 128
TILE = 8

GRAV = 9.81
TSTEP = 8.0
CELL = 90.0
FLOOR = 0.05
BANK_COEF = 200.0
CELL_AREA = 8100.0
NODE_AREA = 20000.0

SLOPE = GRAV * TSTEP / CELL
LEVEL = SLOPE * TSTEP / CELL
FLOW = LEVEL * TSTEP / CELL
ROUGH = math.sqrt(0.25 * GRAV * TSTEP * LEVEL ** (7.0 / 3.0) / FLOW)
KEEP = 1.0 - TSTEP * BANK_COEF * 4.0 / NODE_AREA
GAIN = TSTEP * BANK_COEF / NODE_AREA
INTO = TSTEP * BANK_COEF / CELL_AREA

MESH = pl.DeviceIdType.MESH
VMEM_BYTES = 24 * 1024 * 1024
FAR = -(1 << 24)
OFFSETS = (-1, 1, -2, 2)


def wave(batches):
    running, waiting = [], list(batches)
    while running or waiting:
        if waiting:
            running.extend(waiting.pop(0))
        for unit in list(running):
            try:
                next(unit)
            except StopIteration:
                running.remove(unit)


def by(size, units):
    units = list(units)
    return [units[i : i + size] for i in range(0, len(units), size)]


def halves(value):
    high = value.astype(jnp.bfloat16)
    return high, (value - high.astype(jnp.float32)).astype(jnp.bfloat16)


def flood_kernel(
    table_in,
    depth_in,
    east_in,
    south_in,
    bed_in,
    rough_in,
    section_in,
    cells_in,
    depth_out,
    east_out,
    south_out,
    section_out,
    table,
    raw,
    raw_rough,
    edge,
    edge_rough,
    far,
    far_rough,
    tops,
    bottoms,
    surf,
    fe,
    fs,
    bed,
    mann,
    max_e,
    max_s,
    drag_e,
    drag_s,
    tally,
    number,
    number4,
    boxes,
    partial,
    sections,
    cells,
    part,
    low,
    high,
    in_sem,
    strip_ssem,
    strip_rsem,
    node_ssem,
    node_rsem,
    part_ssem,
    part_rsem,
):
    me = lax.axis_index("gy")
    tiles = lax.axis_size("gy")
    rows, columns = depth_in.shape
    ext = rows + 2 * HALO
    chunks = columns // LANES
    owned = section_in.shape[1]
    total = 5 * owned

    def there(offset):
        return (me + offset >= 0) & (me + offset < tiles)

    def absent(offset):
        return jnp.logical_not(there(offset))

    barrier = pltpu.get_barrier_semaphore()
    for offset in OFFSETS:
        @pl.when(there(offset))
        def _():
            pl.semaphore_signal(
                barrier, inc=1, device_id={"gy": me + offset}, device_id_type=MESH
            )

    fields = (depth_in, bed_in, east_in, south_in)
    loads = [
        pltpu.make_async_copy(source, target, in_sem.at[i])
        for i, (source, target) in enumerate(
            [(field, raw.at[i]) for i, field in enumerate(fields)]
            + [
                (rough_in, raw_rough),
                (table_in, table),
                (section_in, sections.at[2]),
                (cells_in, cells.at[2]),
            ]
        )
    ]
    for load in loads:
        load.start()

    def send(src, dst, ssem, rsem, offset):
        return pltpu.make_async_remote_copy(
            src_ref=src,
            dst_ref=dst,
            send_sem=ssem,
            recv_sem=rsem,
            device_id={"gy": me + offset},
            device_id_type=MESH,
        )

    node_sends = {}
    for i, offset in enumerate(OFFSETS):
        slot = 2 - offset
        node_sends[offset] = (
            send(section_in, sections.at[slot], node_ssem.at[0, i], node_rsem.at[0, i], offset),
            send(cells_in, cells.at[slot], node_ssem.at[1, i], node_rsem.at[1, i], offset),
        )
    strip_sends, far_sends = {}, {}
    for i, offset in enumerate((-1, 1)):
        for group, (first, stop) in enumerate(((0, SOON), (SOON, HALO))):
            if offset < 0:
                theirs, lands = slice(first, stop), slice(first, stop)
            else:
                theirs = slice(rows - stop, rows - first)
                lands = slice(2 * HALO - stop, 2 * HALO - first)
            there_f, there_r = ((edge, edge_rough), (far, far_rough))[group]
            sources = [field.at[theirs] for field in fields] + [rough_in.at[theirs]]
            targets = [there_f.at[j, lands] for j in range(4)] + [there_r.at[lands]]
            (strip_sends, far_sends)[group][offset] = [
                send(
                    source,
                    target,
                    strip_ssem.at[i, 5 * group + j],
                    strip_rsem.at[i, 5 * group + j],
                    offset,
                )
                for j, (source, target) in enumerate(zip(sources, targets))
            ]

    pl.semaphore_wait(barrier, jnp.minimum(me, 2) + jnp.minimum(tiles - 1 - me, 2))
    for offset in OFFSETS:
        @pl.when(there(offset))
        def _():
            for copy in node_sends[offset]:
                copy.start()

    for sends in (strip_sends, far_sends):
        for offset in (-1, 1):
            @pl.when(there(offset))
            def _():
                for copy in sends[offset]:
                    copy.start()

    later = slice(SOON, 2 * HALO - SOON)
    edge[:, later, :] = jnp.zeros((4, 2 * (HALO - SOON), columns), jnp.float32)
    edge_rough[later, :] = jnp.zeros((2 * (HALO - SOON), columns), jnp.int32)

    for load in loads:
        load.wait()

    scaled = [table[k] * ROUGH for k in range(table.shape[0])]

    def roughness(rough):
        values, bit = scaled, 1
        while len(values) > 1:
            odd = (rough & bit) != 0
            values = [
                jnp.where(odd, values[i + 1], values[i]) if i + 1 < len(values) else values[i]
                for i in range(0, len(values), 2)
            ]
            bit *= 2
        return values[0]

    def at(c):
        return slice(LANES * c, LANES * (c + 1))

    lane_id = lax.broadcasted_iota(jnp.int32, (1, LANES), 1)

    def turn(value, shift):
        return pltpu.roll(value, LANES - shift, 1)

    def lanes_to(value, preceding, shift):
        mixed = jnp.where(lane_id < LANES - shift, value, preceding)
        return pltpu.roll(mixed, shift, 1)

    def south(value):
        return pltpu.roll(value, value.shape[0] - 1, 0)

    def north(value):
        return pltpu.roll(value, 1, 0)

    row_id = lax.broadcasted_iota(jnp.int32, (TILE, LANES), 0)
    shut_last = (row_id == TILE - 1) & (me == tiles - 1)
    shut_first = (row_id == TILE - 1) & (me == 0)

    def depth_of(surf_a, surf_b, bed_top):
        return jnp.maximum(jnp.maximum(surf_a, surf_b) - bed_top, FLOOR * LEVEL)

    def power_log(flow_depth):
        return lax.log2(flow_depth) * (-7.0 / 3.0)

    def damping(flux, drag, power):
        return 1.0 / (1.0 + drag * jnp.abs(flux) * power)

    def square(value):
        return value * value

    def closed_east(c, flux):
        return jnp.where(lane_id == LANES - 1, 0.0, flux) if c == chunks - 1 else flux

    def closed_south(flux):
        count = flux.shape[0]
        return jnp.concatenate(
            [flux[: count - 2 * TILE]] * (count > 2 * TILE)
            + [
                jnp.where(shut_last, 0.0, flux[count - 2 * TILE : count - TILE]),
                jnp.where(shut_first, 0.0, flux[count - TILE :]),
            ],
            axis=0,
        )

    def last_four(value, carried):
        pair = value + lanes_to(value, carried[0], 1)
        return pair + lanes_to(pair, carried[1], 2), (value, pair)

    def zeros(count):
        return jnp.zeros((count, LANES), jnp.float32)

    after = {}

    def put(name, c, value):
        after[name, c] = value

    def got(name, c, count):
        return after.get((name, c), zeros(count))

    def two_on(name, c, count):
        return jnp.where(lane_id < LANES - 2, after[name, c], got(name, c + 1, count))

    inner = rows - TILE

    def own_chunk(c):
        floor = raw[1, :, at(c)] * LEVEL
        bed[:rows, at(c)] = floor
        mine = roughness(raw_rough[:, at(c)])
        mann[:rows, at(c)] = mine
        here = raw[0, :, at(c)] * LEVEL + floor
        surf[:rows, at(c)] = here
        tops[0, :, at(c)] = here[:TILE]
        turned = [turn(a, 1) for a in (here, floor, mine)]
        put("own", c, (here, turned))
        yield
        yield
        following = after.get(("own", c + 1), (zeros(rows), [zeros(rows)] * 3))
        east, floor_e, mann_e = (
            jnp.where(lane_id < LANES - 1, a, b) for a, b in zip(turned, following[1])
        )
        pair = here + east
        put("pair", c, turn(pair, 2))
        top = jnp.maximum(floor, floor_e)
        drag = square(mine + mann_e)
        max_e[:rows, at(c)] = top
        drag_e[:rows, at(c)] = drag
        depth_e = depth_of(here, east, top)
        log_e = power_log(depth_e)
        below_s = south(here)[:inner]
        top = jnp.maximum(floor, south(floor))[:inner]
        drag_b = square((mine + south(mine))[:inner])
        max_s[:inner, at(c)] = top
        drag_s[:inner, at(c)] = drag_b
        depth_s = depth_of(here[:inner], below_s, top)
        log_s = power_log(depth_s)
        yield
        power_e, power_s = jnp.exp2(log_e), jnp.exp2(log_s)
        flux_e = raw[2, :, at(c)] * FLOW
        flux_s = raw[3, :inner, at(c)] * FLOW
        yield
        boxes[:rows, at(c)] = pair + two_on("pair", c, rows)
        damp_e = damping(flux_e, drag, power_e)
        damp_s = damping(flux_s, drag_b, power_s)
        yield
        new_east = closed_east(c, (flux_e - depth_e * (east - here)) * damp_e)
        new_south = (flux_s - depth_s * (below_s - here[:inner])) * damp_s
        fe[:rows, at(c)] = new_east
        fs[:inner, at(c)] = new_south
        put("east", c, new_east)
        west = lanes_to(new_east, got("east", c - 1, rows), 1)
        yield
        partial[:, at(c)] = here + (west - new_east)

    wave(by(2, (own_chunk(c) for c in range(chunks))))
    after.clear()

    def nodes_of(offsets):
        for offset in offsets:
            @pl.when(there(-offset))
            def _():
                for copy in node_sends[offset]:
                    copy.wait_recv()

            @pl.when(absent(-offset))
            def _():
                sections[2 - offset] = jnp.zeros((1, owned), jnp.float32)
                cells[2 - offset] = jnp.full((cells.shape[1], owned), FAR, jnp.int32)

    def one_hot(count, index):
        found = lax.broadcasted_iota(jnp.int32, (count, index.shape[1]), 0) == index
        return jnp.where(found, 1.0, 0.0).astype(jnp.bfloat16)

    def locate(slots):
        section = jnp.concatenate([sections[i] for i in slots], axis=1)
        cell = jnp.concatenate([cells[i, 0:1, :] for i in slots], axis=1)
        local = cell - (me * rows - HALO) * columns
        valid = (local >= 0) & (local < ext * columns)
        local = jnp.where(valid, local, 0)
        from_top = ((local.astype(jnp.float32) + 0.5) * (1.0 / columns)).astype(jnp.int32)
        column = local - from_top * columns
        chunk = column >> 7
        own = valid & (from_top >= HALO) & (from_top < rows + HALO)
        place = jnp.where(own, chunk * rows + from_top - HALO, -1)
        beyond = jnp.where(from_top < HALO, from_top + HALO, from_top - rows - HALO)
        place_edge = jnp.where(valid & jnp.logical_not(own), chunk * TILE + beyond, -1)
        lane = column & (LANES - 1)
        lane_hit = lax.broadcasted_iota(jnp.int32, (LANES, lane.shape[1]), 0) == lane
        levels = section * (LEVEL * INTO)
        level_high = levels.astype(jnp.bfloat16).astype(jnp.float32)
        weights = jnp.concatenate(
            [
                jnp.where(lane_hit, value, 0.0)
                for value in (level_high, levels - level_high, jnp.ones_like(levels))
            ],
            axis=0,
        ).astype(jnp.bfloat16)
        return section, own, place, place_edge, lane_hit, weights

    def spread_by(hits, weights):
        return lax.dot_general(
            hits, weights, (((1,), (1,)), ((), ())), preferred_element_type=jnp.float32
        )

    def planes(block):
        level = block[:, :LANES] + block[:, LANES : 2 * LANES]
        return level, block[:, 2 * LANES :] * INTO

    def share(name, span, c, level, count):
        count4, counted[name] = last_four(count, counted[name])
        tally[span, at(c)] = level
        number[span, at(c)] = count * GAIN
        number4[span, at(c)] = count4

    outer = slice(rows, ext)
    counted = {"own": (zeros(rows),) * 2, "edge": (zeros(TILE),) * 2}
    nodes_of((-1, 1))
    section, own, place, place_edge, lane_hit, weights = locate((1, 2, 3))
    hit = one_hot(chunks * rows, place)
    spread = spread_by(hit, weights)
    for c in range(chunks):
        share("own", slice(0, rows), c, *planes(spread[c * rows : (c + 1) * rows]))

    nodes_of((-2, 2))
    _, _, _, place_more, _, weights_more = locate((0, 4))
    hit_edge = one_hot(
        -(-chunks * TILE // 16) * 16, jnp.concatenate([place_edge, place_more], axis=1)
    )
    spread = spread_by(hit_edge, jnp.concatenate([weights, weights_more], axis=1))
    for c in range(chunks):
        share("edge", outer, c, *planes(spread[c * TILE : (c + 1) * TILE]))

    for i, offset in enumerate((-1, 1)):
        @pl.when(there(-offset))
        def _():
            for copy in strip_sends[offset]:
                copy.wait_recv()

        @pl.when(absent(-offset))
        def _():
            lands = slice(HALO * i, HALO * (i + 1))
            edge[:, lands, :] = jnp.zeros((4, HALO, columns), jnp.float32)
            edge_rough[lands, :] = jnp.zeros((HALO, columns), jnp.int32)

    def edge_chunk(c):
        floor = edge[1, :, at(c)] * LEVEL
        here = edge[0, :, at(c)] * LEVEL + floor
        mine = roughness(edge_rough[:, at(c)])
        turned = [turn(a, 1) for a in (here, floor, mine)]
        put("edge", c, (here, turned))
        yield
        yield
        following = after.get(("edge", c + 1), (zeros(TILE), [zeros(TILE)] * 3))
        east, floor_e, mann_e = (
            jnp.where(lane_id < LANES - 1, a, b) for a, b in zip(turned, following[1])
        )
        pair = here + east
        put("edge_pair", c, turn(pair, 2))
        top = jnp.maximum(floor, floor_e)
        drag = square(mine + mann_e)
        max_e[outer, at(c)] = top
        drag_e[outer, at(c)] = drag
        depth_e = depth_of(here, east, top)
        log_e = power_log(depth_e)
        whole = jnp.concatenate([surf[:rows, at(c)], here], axis=0)
        below_s = south(whole)[inner:]
        floor = jnp.concatenate([bed[:rows, at(c)], floor], axis=0)
        mine = jnp.concatenate([mann[:rows, at(c)], mine], axis=0)
        top = jnp.maximum(floor, south(floor))[inner:]
        drag_b = square((mine + south(mine))[inner:])
        max_s[inner:, at(c)] = top
        drag_s[inner:, at(c)] = drag_b
        depth_s = depth_of(whole[inner:], below_s, top)
        log_s = power_log(depth_s)
        levels = tally[:, at(c)]
        put("edge_levels", c, levels)
        spill = levels + lanes_to(levels, got("edge_levels", c - 1, ext), 1)
        put("edge_spill", c, spill)
        yield
        spill2 = lanes_to(spill, got("edge_spill", c - 1, ext), 2)
        power_e, power_s = jnp.exp2(log_e), jnp.exp2(log_s)
        flux_e = edge[2, :, at(c)] * FLOW
        flux_s = jnp.concatenate([raw[3, inner:, at(c)], edge[3, :, at(c)]], axis=0) * FLOW
        yield
        boxes[outer, at(c)] = pair + two_on("edge_pair", c, TILE)
        damp_e = damping(flux_e, drag, power_e)
        damp_s = damping(flux_s, drag_b, power_s)
        yield
        new_east = closed_east(c, (flux_e - depth_e * (east - here)) * damp_e)
        new_south = closed_south((flux_s - depth_s * (below_s - whole[inner:])) * damp_s)
        fe[outer, at(c)] = new_east
        fs[inner:, at(c)] = new_south
        bottoms[0, :, at(c)] = new_south[:TILE]
        put("edge_east", c, new_east)
        west = lanes_to(new_east, got("edge_east", c - 1, TILE), 1)
        new_south = jnp.concatenate([fs[:inner, at(c)], new_south], axis=0)
        yield
        surf[:, at(c)] = (
            jnp.concatenate([partial[:, at(c)], here + (west - new_east)], axis=0)
            + (north(new_south) - new_south)
            + (spill + spill2 - number4[:, at(c)] * whole)
        )

    def spilled(name, c, moved):
        count = moved.shape[0]
        put((name, 1), c, moved)
        once = moved + lanes_to(moved, got((name, 1), c - 1, count), 1)
        put((name, 2), c, once)
        return lambda: once + lanes_to(once, got((name, 2), c - 1, count), 2)

    def chunk_step(step, c):
        count = rows if step == STEPS - 2 else ext
        span = slice(0, count)
        whole = surf[:, at(c)]
        here = whole[:count]
        tops[step, :, at(c)] = whole[:TILE]
        turned = turn(here, 1)
        put(("here", step), c, (here, turned))
        yield
        yield
        following = after.get((("here", step), c + 1), (zeros(count), zeros(count)))
        east = jnp.where(lane_id < LANES - 1, turned, following[1])
        depth_e = depth_of(here, east, max_e[span, at(c)])
        log_e = power_log(depth_e)
        below_s = south(whole)
        depth_s = depth_of(whole, below_s, max_s[:, at(c)])
        log_s = power_log(depth_s)
        pair = here + east
        put(("pair", step), c, turn(pair, 2))
        box = boxes[span, at(c)]
        spill = spilled(("moved", step), c, number[span, at(c)] * box + KEEP**step * tally[span, at(c)])
        yield
        power_e, power_s = jnp.exp2(log_e), jnp.exp2(log_s)
        source = spill()
        yield
        boxes[span, at(c)] = KEEP * box + (pair + two_on(("pair", step), c, count))
        flux_e, flux_s = fe[span, at(c)], fs[:, at(c)]
        damp_e = damping(flux_e, drag_e[span, at(c)], power_e)
        damp_s = damping(flux_s, drag_s[:, at(c)], power_s)
        source = source - number4[span, at(c)] * here
        yield
        new_east = closed_east(c, (flux_e - depth_e * (east - here)) * damp_e)
        new_south = closed_south((flux_s - depth_s * (below_s - whole)) * damp_s)
        put(("east", step), c, new_east)
        west = lanes_to(new_east, got(("east", step), c - 1, count), 1)
        fe[span, at(c)] = new_east
        fs[span, at(c)] = new_south[:count]
        bottoms[step, :, at(c)] = new_south[inner:rows]
        yield
        level = here + (west - new_east) + (north(new_south) - new_south)[:count] + source
        surf[span, at(c)] = level

    def halo_step(step, c):
        if step == 0:
            floor = edge[1, :, at(c)] * LEVEL
            here = edge[0, :, at(c)] * LEVEL + floor
            mine = roughness(edge_rough[:, at(c)])
            turned = [turn(a, 1) for a in (here, floor, mine)]
        else:
            here = surf[outer, at(c)]
            turned = [turn(here, 1)]
        put(("halo", step), c, turned)
        yield
        yield
        following = after.get((("halo", step), c + 1), [zeros(TILE)] * 3)
        nexts = [jnp.where(lane_id < LANES - 1, a, b) for a, b in zip(turned, following)]
        east = nexts[0]
        pair = here + east
        put(("halo_pair", step), c, turn(pair, 2))

        def southward(value, top):
            return south(jnp.concatenate([value, top], axis=0))[:TILE]

        below_s = southward(here, tops[step, :, at(c)])
        if step == 0:
            top = jnp.maximum(floor, nexts[1])
            drag = square(mine + nexts[2])
            top_s = jnp.maximum(floor, southward(floor, bed[:TILE, at(c)]))
            drag_b = square(mine + southward(mine, mann[:TILE, at(c)]))
            max_e[outer, at(c)] = top
            drag_e[outer, at(c)] = drag
            max_s[outer, at(c)] = top_s
            drag_s[outer, at(c)] = drag_b
            flux_e, flux_s = (edge[i, :, at(c)] * FLOW for i in (2, 3))
            moved = tally[outer, at(c)]
        else:
            top, drag = max_e[outer, at(c)], drag_e[outer, at(c)]
            top_s, drag_b = max_s[outer, at(c)], drag_s[outer, at(c)]
            flux_e, flux_s = fe[outer, at(c)], fs[outer, at(c)]
            box = boxes[outer, at(c)]
            moved = number[outer, at(c)] * box + KEEP**step * tally[outer, at(c)]
        depth_e = depth_of(here, east, top)
        log_e = power_log(depth_e)
        depth_s = depth_of(here, below_s, top_s)
        log_s = power_log(depth_s)
        spill = spilled(("halo_moved", step), c, moved)
        yield
        power_e, power_s = jnp.exp2(log_e), jnp.exp2(log_s)
        source = spill()
        yield
        total = pair + two_on(("halo_pair", step), c, TILE)
        boxes[outer, at(c)] = total if step == 0 else KEEP * box + total
        damp_e = damping(flux_e, drag, power_e)
        damp_s = damping(flux_s, drag_b, power_s)
        source = source - number4[outer, at(c)] * here
        yield
        new_east = closed_east(c, (flux_e - depth_e * (east - here)) * damp_e)
        new_south = (flux_s - depth_s * (below_s - here)) * damp_s
        new_south = jnp.where(shut_first, 0.0, new_south)
        put(("halo_east", step), c, new_east)
        west = lanes_to(new_east, got(("halo_east", step), c - 1, TILE), 1)
        fe[outer, at(c)] = new_east
        fs[outer, at(c)] = new_south
        yield
        into = north(jnp.concatenate([bottoms[step, :, at(c)], new_south], axis=0))[TILE:]
        surf[outer, at(c)] = here + (west - new_east) + (into - new_south) + source

    def last_chunk(c):
        step = STEPS - 1
        here = surf[:rows, at(c)]
        turned = turn(here, 1)
        put("last", c, turned)
        yield
        yield
        east = jnp.where(lane_id < LANES - 1, turned, got("last", c + 1, rows))
        depth_e = depth_of(here, east, max_e[:rows, at(c)])
        log_e = power_log(depth_e)
        below_s = south(here)[:inner]
        depth_s = depth_of(here[:inner], below_s, max_s[:inner, at(c)])
        log_s = power_log(depth_s)
        spill = spilled(
            "last_moved",
            c,
            number[:rows, at(c)] * boxes[:rows, at(c)] + KEEP**step * tally[:rows, at(c)],
        )
        yield
        power_e, power_s = jnp.exp2(log_e), jnp.exp2(log_s)
        source = spill()
        yield
        flux_e, flux_s = fe[:rows, at(c)], fs[:inner, at(c)]
        damp_e = damping(flux_e, drag_e[:rows, at(c)], power_e)
        damp_s = damping(flux_s, drag_s[:inner, at(c)], power_s)
        source = source - number4[:rows, at(c)] * here
        yield
        new_east = closed_east(c, (flux_e - depth_e * (east - here)) * damp_e)
        new_south = (flux_s - depth_s * (below_s - here[:inner])) * damp_s
        put("last_east", c, new_east)
        west = lanes_to(new_east, got("last_east", c - 1, rows), 1)
        east_out[:, at(c)] = new_east * (1.0 / FLOW)
        south_out[:inner, at(c)] = new_south * (1.0 / FLOW)
        fs[:inner, at(c)] = new_south
        yield
        partial[:, at(c)] = here + (west - new_east) + source

    def last_edge(c):
        whole = jnp.concatenate(
            [surf[inner:, at(c)], surf[:TILE, at(c)]], axis=0
        )
        here = whole[: 2 * TILE]
        below_s = south(whole)[: 2 * TILE]
        depth_s = depth_of(here, below_s, max_s[inner:, at(c)])
        log_s = power_log(depth_s)
        yield
        power_s = jnp.exp2(log_s)
        flux_s = fs[inner:, at(c)]
        yield
        damp_s = damping(flux_s, drag_s[inner:, at(c)], power_s)
        yield
        new_south = closed_south((flux_s - depth_s * (below_s - here)) * damp_s)
        south_out[inner:, at(c)] = new_south[:TILE] * (1.0 / FLOW)
        new_south = jnp.concatenate([fs[:inner, at(c)], new_south], axis=0)
        level = partial[:, at(c)] + (north(new_south) - new_south)[:rows]
        depth_out[:, at(c)] = level * (1.0 / LEVEL) - raw[1, :, at(c)]

    flat = {}

    def node_chunk(c):
        here = surf[:rows, at(c)]
        turned = turn(here, 1)
        put("node", c, (here, turned))
        yield
        yield
        following = after.get(("node", c + 1), (zeros(rows), zeros(rows)))
        pair = here + jnp.where(lane_id < LANES - 1, turned, following[1])
        put("node_pair", c, turn(pair, 2))
        yield
        yield
        flat[c] = KEEP * boxes[:rows, at(c)] + (pair + two_on("node_pair", c, rows))

    batches = by(5, (edge_chunk(c) for c in range(chunks))) + [[]] * 3
    for step in range(1, STEPS - 1):
        batches += by(3, (chunk_step(step, c) for c in range(chunks))) + [[]]
    wave(batches + [[]] * 2 + by(5, (node_chunk(c) for c in range(chunks))))
    flat = [flat[c] for c in range(chunks)]

    turned = jnp.concatenate(halves(jnp.concatenate(flat, axis=0).T), axis=0)
    picked = jnp.dot(turned, hit, preferred_element_type=jnp.float32)
    picked = picked[:LANES] + picked[LANES:]
    picked = jnp.sum(jnp.where(lane_hit, picked, 0.0), axis=0, keepdims=True)
    final = jnp.where(
        own, KEEP**STEPS * section + (GAIN / LEVEL) * picked, 0.0
    )
    for i in range(3):
        part[i] = final[:, i * owned : (i + 1) * owned]

    part_prev = send(part.at[0], high, part_ssem.at[0], part_rsem.at[0], -1)
    part_next = send(part.at[2], low, part_ssem.at[1], part_rsem.at[1], 1)

    @pl.when(there(-1))
    def _():
        part_prev.start()

    @pl.when(there(1))
    def _():
        part_next.start()

    for i, offset in enumerate((-1, 1)):
        @pl.when(there(-offset))
        def _():
            for copy in far_sends[offset]:
                copy.wait_recv()

            row = HALO - 1 + i
            edge[:, row : row + 1, :] = far[:, row : row + 1, :]
            edge_rough[row : row + 1, :] = far_rough[row : row + 1, :]

    lasting = by(3, (last_chunk(c) for c in range(chunks)))
    batches = []
    for step in range(STEPS - 1):
        batches += by(5, (halo_step(step, c) for c in range(chunks))) + [[]] * 4
    for i, batch in enumerate(lasting):
        batches[i + 3] = batches[i + 3] + batch
    wave(batches + by(5, (last_edge(c) for c in range(chunks))))

    for offset in OFFSETS:
        @pl.when(there(offset))
        def _():
            for copy in node_sends[offset]:
                copy.wait_send()

    for offset in (-1, 1):
        @pl.when(there(offset))
        def _():
            for copy in strip_sends[offset] + far_sends[offset]:
                copy.wait_send()

    section_out[...] = part[1]

    @pl.when(there(1))
    def _():
        part_prev.wait_recv()
        section_out[...] += high[...]

    @pl.when(there(-1))
    def _():
        part_next.wait_recv()
        section_out[...] += low[...]

    @pl.when(there(-1))
    def _():
        part_prev.wait_send()

    @pl.when(there(1))
    def _():
        part_next.wait_send()


def finish_kernel(a, b, c, d, a_out, b_out, c_out, d_out, out_sem):
    stores = [
        pltpu.make_async_copy(source, target, out_sem.at[i])
        for i, (source, target) in enumerate(
            ((a, a_out), (b, b_out), (c, c_out), (d, d_out))
        )
    ]
    for store in stores:
        store.start()
    for store in stores:
        store.wait()


def finish(*arrays):
    return pl.pallas_call(
        finish_kernel,
        out_shape=[jax.ShapeDtypeStruct(a.shape, a.dtype) for a in arrays],
        in_specs=[pl.BlockSpec(memory_space=pltpu.VMEM)] * 4,
        out_specs=[pl.BlockSpec(memory_space=pltpu.MemorySpace.HBM)] * 4,
        scratch_shapes=[pltpu.SemaphoreType.DMA((4,))],
        compiler_params=pltpu.CompilerParams(vmem_limit_bytes=VMEM_BYTES),
        name="finish",
    )(*arrays)


def local(
    depth, flux_east, flux_south, river_section, bed_level, rough_class, manning_table, bank_cell
):
    rows, columns = depth.shape
    owned = river_section.shape[0]
    width, _ = bank_cell.shape
    ext = rows + 2 * HALO
    operands = [
        pltpu.with_memory_space_constraint(a, pltpu.MemorySpace.HBM)
        for a in (
            manning_table,
            depth,
            flux_east,
            flux_south,
            bed_level,
            rough_class,
            river_section.reshape(1, owned),
            bank_cell,
        )
    ]
    hbm = pl.BlockSpec(memory_space=pltpu.MemorySpace.HBM)
    vmem = pl.BlockSpec(memory_space=pltpu.VMEM)
    tile = pltpu.VMEM((rows, columns), jnp.float32)
    line = pltpu.VMEM((1, owned), jnp.float32)
    wide = pltpu.VMEM((ext, columns), jnp.float32)
    dma = pltpu.SemaphoreType.DMA
    depth, flux_east, flux_south, section = pl.pallas_call(
        flood_kernel,
        out_shape=[tile, tile, tile, line],
        in_specs=[hbm] * 8,
        out_specs=[vmem] * 4,
        scratch_shapes=[
            pltpu.SMEM(manning_table.shape, jnp.float32),
            pltpu.VMEM((4, rows, columns), jnp.float32),
            pltpu.VMEM((rows, columns), jnp.int32),
            pltpu.VMEM((4, 2 * HALO, columns), jnp.float32),
            pltpu.VMEM((2 * HALO, columns), jnp.int32),
            pltpu.VMEM((4, 2 * HALO, columns), jnp.float32),
            pltpu.VMEM((2 * HALO, columns), jnp.int32),
            pltpu.VMEM((STEPS - 1, TILE, columns), jnp.float32),
            pltpu.VMEM((STEPS - 1, TILE, columns), jnp.float32),
        ]
        + [wide] * 13
        + [
            tile,
            pltpu.VMEM((5, 1, owned), jnp.float32),
            pltpu.VMEM((5, width, owned), jnp.int32),
            pltpu.VMEM((3, 1, owned), jnp.float32),
            line,
            line,
            dma((8,)),
            dma((2, 10)),
            dma((2, 10)),
            dma((2, 4)),
            dma((2, 4)),
            dma((2,)),
            dma((2,)),
        ],
        compiler_params=pltpu.CompilerParams(
            collective_id=0, has_side_effects=True, vmem_limit_bytes=VMEM_BYTES
        ),
        name="flood",
    )(*operands)
    depth, flux_east, flux_south, section = finish(depth, flux_east, flux_south, section)
    return depth, flux_east, flux_south, section.reshape(owned)


def solution(mesh):
    return jax.shard_map(
        local,
        mesh=mesh,
        in_specs=(
            P(("runs", "gy"), None),
            P(("runs", "gy"), None),
            P(("runs", "gy"), None),
            P(("runs", "gy")),
            P("gy", None),
            P("gy", None),
            P(),
            P(None, "gy"),
        ),
        out_specs=(
            P(("runs", "gy"), None),
            P(("runs", "gy"), None),
            P(("runs", "gy"), None),
            P(("runs", "gy")),
        ),
        check_vma=False,
    )
```

```python
import math

import jax
import jax.numpy as jnp
from jax import lax
from jax.experimental import pallas as pl
from jax.experimental.pallas import tpu as pltpu
from jax.sharding import PartitionSpec as P

STEPS = 4
HALO = STEPS
TIERS = ((0, 2), (2, 3), (3, 4))
LANES = 128
TILE = 8

GRAV = 9.81
TSTEP = 8.0
CELL = 90.0
FLOOR = 0.05
BANK_COEF = 200.0
CELL_AREA = 8100.0
NODE_AREA = 20000.0

SLOPE = GRAV * TSTEP / CELL
LEVEL = SLOPE * TSTEP / CELL
FLOW = LEVEL * TSTEP / CELL
ROUGH = math.sqrt(0.25 * GRAV * TSTEP * LEVEL ** (7.0 / 3.0) / FLOW)
KEEP = 1.0 - TSTEP * BANK_COEF * 4.0 / NODE_AREA
GAIN = TSTEP * BANK_COEF / NODE_AREA
INTO = TSTEP * BANK_COEF / CELL_AREA

MESH = pl.DeviceIdType.MESH
VMEM_BYTES = 24 * 1024 * 1024
FAR = -(1 << 24)
OFFSETS = (-1, 1, -2, 2)


def wave(batches):
    running, waiting = [], list(batches)
    while running or waiting:
        if waiting:
            running.extend(waiting.pop(0))
        for unit in list(running):
            try:
                next(unit)
            except StopIteration:
                running.remove(unit)


def by(size, units):
    units = list(units)
    return [units[i : i + size] for i in range(0, len(units), size)]


def halves(value):
    high = value.astype(jnp.bfloat16)
    return high, (value - high.astype(jnp.float32)).astype(jnp.bfloat16)


def flood_kernel(
    table_in,
    depth_in,
    east_in,
    south_in,
    bed_in,
    rough_in,
    section_in,
    cells_in,
    depth_out,
    east_out,
    south_out,
    section_out,
    table,
    raw,
    raw_rough,
    edge,
    edge_rough,
    far,
    far_rough,
    tops,
    bottoms,
    surf,
    fe,
    fs,
    bed,
    mann,
    max_e,
    max_s,
    drag_e,
    drag_s,
    tally,
    number,
    number4,
    boxes,
    partial,
    sections,
    cells,
    part,
    low,
    high,
    in_sem,
    strip_ssem,
    strip_rsem,
    node_ssem,
    node_rsem,
    part_ssem,
    part_rsem,
):
    me = lax.axis_index("gy")
    tiles = lax.axis_size("gy")
    rows, columns = depth_in.shape
    ext = rows + 2 * HALO
    chunks = columns // LANES
    owned = section_in.shape[1]
    total = 5 * owned

    def there(offset):
        return (me + offset >= 0) & (me + offset < tiles)

    def absent(offset):
        return jnp.logical_not(there(offset))

    edge[...] = jnp.zeros(edge.shape, jnp.float32)
    edge_rough[...] = jnp.zeros(edge_rough.shape, jnp.int32)
    barrier = pltpu.get_barrier_semaphore()
    for offset in OFFSETS:
        @pl.when(there(offset))
        def _():
            pl.semaphore_signal(
                barrier, inc=1, device_id={"gy": me + offset}, device_id_type=MESH
            )

    fields = (depth_in, bed_in, east_in, south_in)
    loads = [
        pltpu.make_async_copy(source, target, in_sem.at[i])
        for i, (source, target) in enumerate(
            [(field, raw.at[i]) for i, field in enumerate(fields)]
            + [
                (rough_in, raw_rough),
                (table_in, table),
                (section_in, sections.at[2]),
                (cells_in, cells.at[2]),
            ]
        )
    ]
    for load in loads:
        load.start()

    def send(src, dst, ssem, rsem, offset):
        return pltpu.make_async_remote_copy(
            src_ref=src,
            dst_ref=dst,
            send_sem=ssem,
            recv_sem=rsem,
            device_id={"gy": me + offset},
            device_id_type=MESH,
        )

    node_sends = {}
    for i, offset in enumerate(OFFSETS):
        slot = 2 - offset
        node_sends[offset] = (
            send(section_in, sections.at[slot], node_ssem.at[0, i], node_rsem.at[0, i], offset),
            send(cells_in, cells.at[slot], node_ssem.at[1, i], node_rsem.at[1, i], offset),
        )
    def span_of(tier, field, offset):
        first, stop = TIERS[tier]
        if field == 2 or (field == 3 and offset < 0):
            return max(first - 1, 0), stop - 1
        return first, stop

    def landing(tier, field, offset):
        first, stop = span_of(tier, field, offset)
        return slice(first, stop) if offset < 0 else slice(2 * HALO - stop, 2 * HALO - first)

    strip_sends = {}
    for i, offset in enumerate((-1, 1)):
        for tier in range(len(TIERS)):
            strip_sends[tier, offset] = []
            for j in range(5):
                first, stop = span_of(tier, j, offset)
                theirs = slice(first, stop) if offset < 0 else slice(rows - stop, rows - first)
                lands = landing(tier, j, offset)
                if j < 4:
                    source = fields[j].at[theirs]
                    target = edge.at[j, lands] if tier == 0 else far.at[tier - 1, j, lands]
                else:
                    source = rough_in.at[theirs]
                    target = edge_rough.at[lands] if tier == 0 else far_rough.at[tier - 1, lands]
                sem = 5 * tier + j
                strip_sends[tier, offset].append(
                    send(source, target, strip_ssem.at[i, sem], strip_rsem.at[i, sem], offset)
                )

    pl.semaphore_wait(barrier, jnp.minimum(me, 2) + jnp.minimum(tiles - 1 - me, 2))
    for offset in OFFSETS:
        @pl.when(there(offset))
        def _():
            for copy in node_sends[offset]:
                copy.start()

    for tier in range(len(TIERS)):
        for offset in (-1, 1):
            @pl.when(there(offset))
            def _():
                for copy in strip_sends[tier, offset]:
                    copy.start()

    for load in loads:
        load.wait()

    scaled = [table[k] * ROUGH for k in range(table.shape[0])]

    def roughness(rough):
        values, bit = scaled, 1
        while len(values) > 1:
            odd = (rough & bit) != 0
            values = [
                jnp.where(odd, values[i + 1], values[i]) if i + 1 < len(values) else values[i]
                for i in range(0, len(values), 2)
            ]
            bit *= 2
        return values[0]

    def at(c):
        return slice(LANES * c, LANES * (c + 1))

    lane_id = lax.broadcasted_iota(jnp.int32, (1, LANES), 1)

    def turn(value, shift):
        return pltpu.roll(value, LANES - shift, 1)

    def lanes_to(value, preceding, shift):
        mixed = jnp.where(lane_id < LANES - shift, value, preceding)
        return pltpu.roll(mixed, shift, 1)

    def south(value):
        return pltpu.roll(value, value.shape[0] - 1, 0)

    def north(value):
        return pltpu.roll(value, 1, 0)

    row_id = lax.broadcasted_iota(jnp.int32, (TILE, LANES), 0)
    shut_last = (row_id == TILE - 1) & (me == tiles - 1)
    shut_first = (row_id == TILE - 1) & (me == 0)

    def depth_of(surf_a, surf_b, bed_top):
        return jnp.maximum(jnp.maximum(surf_a, surf_b) - bed_top, FLOOR * LEVEL)

    def power_log(flow_depth):
        return lax.log2(flow_depth) * (-7.0 / 3.0)

    def damping(flux, drag, power):
        return 1.0 / (1.0 + drag * jnp.abs(flux) * power)

    def square(value):
        return value * value

    def closed_east(c, flux):
        return jnp.where(lane_id == LANES - 1, 0.0, flux) if c == chunks - 1 else flux

    def closed_south(flux):
        count = flux.shape[0]
        return jnp.concatenate(
            [flux[: count - 2 * TILE]] * (count > 2 * TILE)
            + [
                jnp.where(shut_last, 0.0, flux[count - 2 * TILE : count - TILE]),
                jnp.where(shut_first, 0.0, flux[count - TILE :]),
            ],
            axis=0,
        )

    def last_four(value, carried):
        pair = value + lanes_to(value, carried[0], 1)
        return pair + lanes_to(pair, carried[1], 2), (value, pair)

    def zeros(count):
        return jnp.zeros((count, LANES), jnp.float32)

    after = {}

    def put(name, c, value):
        after[name, c] = value

    def got(name, c, count):
        return after.get((name, c), zeros(count))

    def two_on(name, c, count):
        return jnp.where(lane_id < LANES - 2, after[name, c], got(name, c + 1, count))

    inner = rows - TILE

    def own_chunk(c):
        floor = raw[1, :, at(c)] * LEVEL
        bed[:rows, at(c)] = floor
        mine = roughness(raw_rough[:, at(c)])
        mann[:rows, at(c)] = mine
        here = raw[0, :, at(c)] * LEVEL + floor
        surf[:rows, at(c)] = here
        tops[0, :, at(c)] = here[:TILE]
        turned = [turn(a, 1) for a in (here, floor, mine)]
        put("own", c, (here, turned))
        yield
        yield
        following = after.get(("own", c + 1), (zeros(rows), [zeros(rows)] * 3))
        east, floor_e, mann_e = (
            jnp.where(lane_id < LANES - 1, a, b) for a, b in zip(turned, following[1])
        )
        pair = here + east
        put("pair", c, turn(pair, 2))
        top = jnp.maximum(floor, floor_e)
        drag = square(mine + mann_e)
        max_e[:rows, at(c)] = top
        drag_e[:rows, at(c)] = drag
        depth_e = depth_of(here, east, top)
        log_e = power_log(depth_e)
        below_s = south(here)[:inner]
        top = jnp.maximum(floor, south(floor))[:inner]
        drag_b = square((mine + south(mine))[:inner])
        max_s[:inner, at(c)] = top
        drag_s[:inner, at(c)] = drag_b
        depth_s = depth_of(here[:inner], below_s, top)
        log_s = power_log(depth_s)
        yield
        power_e, power_s = jnp.exp2(log_e), jnp.exp2(log_s)
        flux_e = raw[2, :, at(c)] * FLOW
        flux_s = raw[3, :inner, at(c)] * FLOW
        yield
        boxes[:rows, at(c)] = pair + two_on("pair", c, rows)
        damp_e = damping(flux_e, drag, power_e)
        damp_s = damping(flux_s, drag_b, power_s)
        yield
        new_east = closed_east(c, (flux_e - depth_e * (east - here)) * damp_e)
        new_south = (flux_s - depth_s * (below_s - here[:inner])) * damp_s
        fe[:rows, at(c)] = new_east
        fs[:inner, at(c)] = new_south
        put("east", c, new_east)
        west = lanes_to(new_east, got("east", c - 1, rows), 1)
        yield
        partial[:, at(c)] = here + (west - new_east)

    wave(by(2, (own_chunk(c) for c in range(chunks))))
    after.clear()

    def nodes_of(offsets):
        for offset in offsets:
            @pl.when(there(-offset))
            def _():
                for copy in node_sends[offset]:
                    copy.wait_recv()

            @pl.when(absent(-offset))
            def _():
                sections[2 - offset] = jnp.zeros((1, owned), jnp.float32)
                cells[2 - offset] = jnp.full((cells.shape[1], owned), FAR, jnp.int32)

    def one_hot(count, index):
        found = lax.broadcasted_iota(jnp.int32, (count, index.shape[1]), 0) == index
        return jnp.where(found, 1.0, 0.0).astype(jnp.bfloat16)

    def locate(slots):
        section = jnp.concatenate([sections[i] for i in slots], axis=1)
        cell = jnp.concatenate([cells[i, 0:1, :] for i in slots], axis=1)
        local = cell - (me * rows - HALO) * columns
        valid = (local >= 0) & (local < ext * columns)
        local = jnp.where(valid, local, 0)
        from_top = ((local.astype(jnp.float32) + 0.5) * (1.0 / columns)).astype(jnp.int32)
        column = local - from_top * columns
        chunk = column >> 7
        own = valid & (from_top >= HALO) & (from_top < rows + HALO)
        place = jnp.where(own, chunk * rows + from_top - HALO, -1)
        beyond = jnp.where(from_top < HALO, from_top + HALO, from_top - rows - HALO)
        place_edge = jnp.where(valid & jnp.logical_not(own), chunk * TILE + beyond, -1)
        lane = column & (LANES - 1)
        lane_hit = lax.broadcasted_iota(jnp.int32, (LANES, lane.shape[1]), 0) == lane
        levels = section * (LEVEL * INTO)
        level_high = levels.astype(jnp.bfloat16).astype(jnp.float32)
        weights = jnp.concatenate(
            [
                jnp.where(lane_hit, value, 0.0)
                for value in (level_high, levels - level_high, jnp.ones_like(levels))
            ],
            axis=0,
        ).astype(jnp.bfloat16)
        return section, own, place, place_edge, lane_hit, weights

    def spread_by(hits, weights):
        return lax.dot_general(
            hits, weights, (((1,), (1,)), ((), ())), preferred_element_type=jnp.float32
        )

    def planes(block):
        level = block[:, :LANES] + block[:, LANES : 2 * LANES]
        return level, block[:, 2 * LANES :] * INTO

    def share(name, span, c, level, count):
        count4, counted[name] = last_four(count, counted[name])
        tally[span, at(c)] = level
        number[span, at(c)] = count * GAIN
        number4[span, at(c)] = count4

    outer = slice(rows, ext)
    counted = {"own": (zeros(rows),) * 2, "edge": (zeros(TILE),) * 2}
    nodes_of((-1, 1))
    section, own, place, place_edge, lane_hit, weights = locate((1, 2, 3))
    hit = one_hot(chunks * rows, place)
    spread = spread_by(hit, weights)
    for c in range(chunks):
        share("own", slice(0, rows), c, *planes(spread[c * rows : (c + 1) * rows]))

    for offset in (-1, 1):
        @pl.when(there(-offset))
        def _():
            for copy in strip_sends[0, offset]:
                copy.wait_recv()

    def edge_chunk(c):
        floor = edge[1, :, at(c)] * LEVEL
        here = edge[0, :, at(c)] * LEVEL + floor
        mine = roughness(edge_rough[:, at(c)])
        turned = [turn(a, 1) for a in (here, floor, mine)]
        put("edge", c, (here, turned))
        yield
        yield
        following = after.get(("edge", c + 1), (zeros(TILE), [zeros(TILE)] * 3))
        east, floor_e, mann_e = (
            jnp.where(lane_id < LANES - 1, a, b) for a, b in zip(turned, following[1])
        )
        top = jnp.maximum(floor, floor_e)
        drag = square(mine + mann_e)
        max_e[outer, at(c)] = top
        drag_e[outer, at(c)] = drag
        depth_e = depth_of(here, east, top)
        log_e = power_log(depth_e)
        whole = jnp.concatenate([surf[:rows, at(c)], here], axis=0)
        below_s = south(whole)[inner:]
        floor = jnp.concatenate([bed[:rows, at(c)], floor], axis=0)
        mine = jnp.concatenate([mann[:rows, at(c)], mine], axis=0)
        top = jnp.maximum(floor, south(floor))[inner:]
        drag_b = square((mine + south(mine))[inner:])
        max_s[inner:, at(c)] = top
        drag_s[inner:, at(c)] = drag_b
        depth_s = depth_of(whole[inner:], below_s, top)
        log_s = power_log(depth_s)
        levels = tally[:rows, at(c)]
        put("edge_levels", c, levels)
        spill = levels + lanes_to(levels, got("edge_levels", c - 1, rows), 1)
        put("edge_spill", c, spill)
        yield
        spill2 = lanes_to(spill, got("edge_spill", c - 1, rows), 2)
        power_e, power_s = jnp.exp2(log_e), jnp.exp2(log_s)
        flux_e = edge[2, :, at(c)] * FLOW
        flux_s = jnp.concatenate([raw[3, inner:, at(c)], edge[3, :, at(c)]], axis=0) * FLOW
        yield
        damp_e = damping(flux_e, drag, power_e)
        damp_s = damping(flux_s, drag_b, power_s)
        yield
        new_east = closed_east(c, (flux_e - depth_e * (east - here)) * damp_e)
        new_south = closed_south((flux_s - depth_s * (below_s - whole[inner:])) * damp_s)
        fe[outer, at(c)] = new_east
        fs[inner:, at(c)] = new_south
        bottoms[0, :, at(c)] = new_south[:TILE]
        put("edge_east", c, new_east)
        west = lanes_to(new_east, got("edge_east", c - 1, TILE), 1)
        new_south = jnp.concatenate([fs[:inner, at(c)], new_south], axis=0)
        yield
        gain_s = north(new_south) - new_south
        surf[:rows, at(c)] = (
            partial[:, at(c)]
            + gain_s[:rows]
            + (spill + spill2 - number4[:rows, at(c)] * whole[:rows])
        )
        surf[outer, at(c)] = here + (west - new_east) + gain_s[rows:]

    def edge_source(c):
        spill = spilled("edge_moved", c, tally[outer, at(c)])
        yield
        source = spill()
        yield
        here = (edge[0, :, at(c)] + edge[1, :, at(c)]) * LEVEL
        surf[outer, at(c)] = surf[outer, at(c)] + (source - number4[outer, at(c)] * here)

    def spilled(name, c, moved):
        count = moved.shape[0]
        put((name, 1), c, moved)
        once = moved + lanes_to(moved, got((name, 1), c - 1, count), 1)
        put((name, 2), c, once)
        return lambda: once + lanes_to(once, got((name, 2), c - 1, count), 2)

    def chunk_step(step, c):
        count = rows
        span = slice(0, count)
        whole = surf[:, at(c)]
        here = whole[:count]
        tops[step, :, at(c)] = whole[:TILE]
        turned = turn(here, 1)
        put(("here", step), c, (here, turned))
        yield
        yield
        following = after.get((("here", step), c + 1), (zeros(count), zeros(count)))
        east = jnp.where(lane_id < LANES - 1, turned, following[1])
        depth_e = depth_of(here, east, max_e[span, at(c)])
        log_e = power_log(depth_e)
        below_s = south(whole)
        depth_s = depth_of(whole, below_s, max_s[:, at(c)])
        log_s = power_log(depth_s)
        pair = here + east
        put(("pair", step), c, turn(pair, 2))
        box = boxes[span, at(c)]
        spill = spilled(("moved", step), c, number[span, at(c)] * box + KEEP**step * tally[span, at(c)])
        yield
        power_e, power_s = jnp.exp2(log_e), jnp.exp2(log_s)
        source = spill()
        yield
        boxes[span, at(c)] = KEEP * box + (pair + two_on(("pair", step), c, count))
        flux_e, flux_s = fe[span, at(c)], fs[:, at(c)]
        damp_e = damping(flux_e, drag_e[span, at(c)], power_e)
        damp_s = damping(flux_s, drag_s[:, at(c)], power_s)
        source = source - number4[span, at(c)] * here
        yield
        new_east = closed_east(c, (flux_e - depth_e * (east - here)) * damp_e)
        new_south = closed_south((flux_s - depth_s * (below_s - whole)) * damp_s)
        put(("east", step), c, new_east)
        west = lanes_to(new_east, got(("east", step), c - 1, count), 1)
        fe[span, at(c)] = new_east
        fs[span, at(c)] = new_south[:count]
        bottoms[step, :, at(c)] = new_south[inner:rows]
        yield
        level = here + (west - new_east) + (north(new_south) - new_south)[:count] + source
        surf[span, at(c)] = level

    def halo_step(step, c):
        if step == 0:
            floor = edge[1, :, at(c)] * LEVEL
            here = edge[0, :, at(c)] * LEVEL + floor
            mine = roughness(edge_rough[:, at(c)])
            turned = [turn(a, 1) for a in (here, floor, mine)]
        else:
            here = surf[outer, at(c)]
            turned = [turn(here, 1)]
        put(("halo", step), c, turned)
        yield
        yield
        following = after.get((("halo", step), c + 1), [zeros(TILE)] * 3)
        nexts = [jnp.where(lane_id < LANES - 1, a, b) for a, b in zip(turned, following)]
        east = nexts[0]
        pair = here + east
        put(("halo_pair", step), c, turn(pair, 2))

        def southward(value, top):
            return south(jnp.concatenate([value, top], axis=0))[:TILE]

        below_s = southward(here, tops[step, :, at(c)])
        if step == 0:
            top = jnp.maximum(floor, nexts[1])
            drag = square(mine + nexts[2])
            top_s = jnp.maximum(floor, southward(floor, bed[:TILE, at(c)]))
            drag_b = square(mine + southward(mine, mann[:TILE, at(c)]))
            max_e[outer, at(c)] = top
            drag_e[outer, at(c)] = drag
            max_s[outer, at(c)] = top_s
            drag_s[outer, at(c)] = drag_b
            flux_e, flux_s = (edge[i, :, at(c)] * FLOW for i in (2, 3))
            moved = tally[outer, at(c)]
        else:
            top, drag = max_e[outer, at(c)], drag_e[outer, at(c)]
            top_s, drag_b = max_s[outer, at(c)], drag_s[outer, at(c)]
            flux_e, flux_s = fe[outer, at(c)], fs[outer, at(c)]
            box = boxes[outer, at(c)]
            moved = number[outer, at(c)] * box + KEEP**step * tally[outer, at(c)]
        depth_e = depth_of(here, east, top)
        log_e = power_log(depth_e)
        depth_s = depth_of(here, below_s, top_s)
        log_s = power_log(depth_s)
        spill = spilled(("halo_moved", step), c, moved)
        yield
        power_e, power_s = jnp.exp2(log_e), jnp.exp2(log_s)
        source = spill()
        yield
        total = pair + two_on(("halo_pair", step), c, TILE)
        boxes[outer, at(c)] = total if step == 0 else KEEP * box + total
        damp_e = damping(flux_e, drag, power_e)
        damp_s = damping(flux_s, drag_b, power_s)
        source = source - number4[outer, at(c)] * here
        yield
        new_east = closed_east(c, (flux_e - depth_e * (east - here)) * damp_e)
        new_south = (flux_s - depth_s * (below_s - here)) * damp_s
        new_south = jnp.where(shut_first, 0.0, new_south)
        put(("halo_east", step), c, new_east)
        west = lanes_to(new_east, got(("halo_east", step), c - 1, TILE), 1)
        fe[outer, at(c)] = new_east
        fs[outer, at(c)] = new_south
        yield
        into = north(jnp.concatenate([bottoms[step, :, at(c)], new_south], axis=0))[TILE:]
        surf[outer, at(c)] = here + (west - new_east) + (into - new_south) + source

    def part_chunk(step, c):
        last = step == STEPS - 1
        here = surf[:rows, at(c)]
        turned = turn(here, 1)
        put(("here", step), c, (here, turned))
        if not last:
            tops[step, :, at(c)] = here[:TILE]
        yield
        yield
        following = after.get((("here", step), c + 1), (zeros(rows), zeros(rows)))
        east = jnp.where(lane_id < LANES - 1, turned, following[1])
        depth_e = depth_of(here, east, max_e[:rows, at(c)])
        log_e = power_log(depth_e)
        below_s = south(here)[:inner]
        depth_s = depth_of(here[:inner], below_s, max_s[:inner, at(c)])
        log_s = power_log(depth_s)
        if not last:
            pair = here + east
            put(("pair", step), c, turn(pair, 2))
        box = boxes[:rows, at(c)]
        spill = spilled(
            ("moved", step), c, number[:rows, at(c)] * box + KEEP**step * tally[:rows, at(c)]
        )
        yield
        power_e, power_s = jnp.exp2(log_e), jnp.exp2(log_s)
        source = spill()
        yield
        if not last:
            boxes[:rows, at(c)] = KEEP * box + (pair + two_on(("pair", step), c, rows))
        flux_e, flux_s = fe[:rows, at(c)], fs[:inner, at(c)]
        damp_e = damping(flux_e, drag_e[:rows, at(c)], power_e)
        damp_s = damping(flux_s, drag_s[:inner, at(c)], power_s)
        source = source - number4[:rows, at(c)] * here
        yield
        new_east = closed_east(c, (flux_e - depth_e * (east - here)) * damp_e)
        new_south = (flux_s - depth_s * (below_s - here[:inner])) * damp_s
        put(("east", step), c, new_east)
        west = lanes_to(new_east, got(("east", step), c - 1, rows), 1)
        fs[:inner, at(c)] = new_south
        if last:
            east_out[:, at(c)] = new_east * (1.0 / FLOW)
            south_out[:inner, at(c)] = new_south * (1.0 / FLOW)
        else:
            fe[:rows, at(c)] = new_east
        yield
        partial[:, at(c)] = here + (west - new_east) + source

    def join_chunk(step, c):
        last = step == STEPS - 1
        whole = jnp.concatenate([surf[inner:, at(c)], surf[:TILE, at(c)]], axis=0)
        here = whole[: 2 * TILE]
        below_s = south(whole)[: 2 * TILE]
        depth_s = depth_of(here, below_s, max_s[inner:, at(c)])
        log_s = power_log(depth_s)
        yield
        power_s = jnp.exp2(log_s)
        flux_s = fs[inner:, at(c)]
        yield
        damp_s = damping(flux_s, drag_s[inner:, at(c)], power_s)
        yield
        new_south = closed_south((flux_s - depth_s * (below_s - here)) * damp_s)
        if last:
            south_out[inner:, at(c)] = new_south[:TILE] * (1.0 / FLOW)
        else:
            fs[inner:rows, at(c)] = new_south[:TILE]
            bottoms[step, :, at(c)] = new_south[:TILE]
        new_south = jnp.concatenate([fs[:inner, at(c)], new_south], axis=0)
        level = partial[:, at(c)] + (north(new_south) - new_south)[:rows]
        if last:
            depth_out[:, at(c)] = level * (1.0 / LEVEL) - raw[1, :, at(c)]
        else:
            surf[:rows, at(c)] = level

    def arrive(tier):
        for offset in (-1, 1):
            @pl.when(there(-offset))
            def _():
                for copy in strip_sends[tier, offset]:
                    copy.wait_recv()

                for j in range(4):
                    lands = landing(tier, j, offset)
                    edge[j, lands, :] = far[tier - 1, j, lands, :]
                lands = landing(tier, 4, offset)
                edge_rough[lands, :] = far_rough[tier - 1, lands, :]

    def again(steps, step, extra):
        batches = []
        for done in range(steps):
            batches += by(5, (halo_step(done, c) for c in range(chunks))) + [[]] * 4
        for i, batch in enumerate(by(3, (part_chunk(step, c) for c in range(chunks)))):
            batches[i + 3] = batches[i + 3] + batch
        wave(batches + by(5, (join_chunk(step, c) for c in range(chunks))) + extra)

    flat = {}

    def node_chunk(c):
        here = surf[:rows, at(c)]
        turned = turn(here, 1)
        put("node", c, (here, turned))
        yield
        yield
        following = after.get(("node", c + 1), (zeros(rows), zeros(rows)))
        pair = here + jnp.where(lane_id < LANES - 1, turned, following[1])
        put("node_pair", c, turn(pair, 2))
        yield
        yield
        flat[c] = KEEP * boxes[:rows, at(c)] + (pair + two_on("node_pair", c, rows))

    wave(by(5, (edge_chunk(c) for c in range(chunks))))

    nodes_of((-2, 2))
    _, _, _, place_more, _, weights_more = locate((0, 4))
    hit_edge = one_hot(
        -(-chunks * TILE // 16) * 16, jnp.concatenate([place_edge, place_more], axis=1)
    )
    spread = spread_by(hit_edge, jnp.concatenate([weights, weights_more], axis=1))
    for c in range(chunks):
        share("edge", outer, c, *planes(spread[c * TILE : (c + 1) * TILE]))
    wave(by(5, (edge_source(c) for c in range(chunks))) + [[]] + by(3, (chunk_step(1, c) for c in range(chunks))))

    arrive(1)
    again(2, 2, by(5, (node_chunk(c) for c in range(chunks))))
    flat = [flat[c] for c in range(chunks)]

    turned = jnp.concatenate(halves(jnp.concatenate(flat, axis=0).T), axis=0)
    picked = jnp.dot(turned, hit, preferred_element_type=jnp.float32)
    picked = picked[:LANES] + picked[LANES:]
    picked = jnp.sum(jnp.where(lane_hit, picked, 0.0), axis=0, keepdims=True)
    final = jnp.where(
        own, KEEP**STEPS * section + (GAIN / LEVEL) * picked, 0.0
    )
    for i in range(3):
        part[i] = final[:, i * owned : (i + 1) * owned]

    part_prev = send(part.at[0], high, part_ssem.at[0], part_rsem.at[0], -1)
    part_next = send(part.at[2], low, part_ssem.at[1], part_rsem.at[1], 1)

    @pl.when(there(-1))
    def _():
        part_prev.start()

    @pl.when(there(1))
    def _():
        part_next.start()

    arrive(2)
    again(3, 3, [])

    for offset in OFFSETS:
        @pl.when(there(offset))
        def _():
            for copy in node_sends[offset]:
                copy.wait_send()

    for offset in (-1, 1):
        @pl.when(there(offset))
        def _():
            for tier in range(len(TIERS)):
                for copy in strip_sends[tier, offset]:
                    copy.wait_send()

    section_out[...] = part[1]

    @pl.when(there(1))
    def _():
        part_prev.wait_recv()
        section_out[...] += high[...]

    @pl.when(there(-1))
    def _():
        part_next.wait_recv()
        section_out[...] += low[...]

    @pl.when(there(-1))
    def _():
        part_prev.wait_send()

    @pl.when(there(1))
    def _():
        part_next.wait_send()


def finish_kernel(a, b, c, d, a_out, b_out, c_out, d_out, out_sem):
    stores = [
        pltpu.make_async_copy(source, target, out_sem.at[i])
        for i, (source, target) in enumerate(
            ((a, a_out), (b, b_out), (c, c_out), (d, d_out))
        )
    ]
    for store in stores:
        store.start()
    for store in stores:
        store.wait()


def finish(*arrays):
    return pl.pallas_call(
        finish_kernel,
        out_shape=[jax.ShapeDtypeStruct(a.shape, a.dtype) for a in arrays],
        in_specs=[pl.BlockSpec(memory_space=pltpu.VMEM)] * 4,
        out_specs=[pl.BlockSpec(memory_space=pltpu.MemorySpace.HBM)] * 4,
        scratch_shapes=[pltpu.SemaphoreType.DMA((4,))],
        compiler_params=pltpu.CompilerParams(vmem_limit_bytes=VMEM_BYTES),
        name="finish",
    )(*arrays)


def local(
    depth, flux_east, flux_south, river_section, bed_level, rough_class, manning_table, bank_cell
):
    rows, columns = depth.shape
    owned = river_section.shape[0]
    width, _ = bank_cell.shape
    ext = rows + 2 * HALO
    operands = [
        pltpu.with_memory_space_constraint(a, pltpu.MemorySpace.HBM)
        for a in (
            manning_table,
            depth,
            flux_east,
            flux_south,
            bed_level,
            rough_class,
            river_section.reshape(1, owned),
            bank_cell,
        )
    ]
    hbm = pl.BlockSpec(memory_space=pltpu.MemorySpace.HBM)
    vmem = pl.BlockSpec(memory_space=pltpu.VMEM)
    tile = pltpu.VMEM((rows, columns), jnp.float32)
    line = pltpu.VMEM((1, owned), jnp.float32)
    wide = pltpu.VMEM((ext, columns), jnp.float32)
    dma = pltpu.SemaphoreType.DMA
    depth, flux_east, flux_south, section = pl.pallas_call(
        flood_kernel,
        out_shape=[tile, tile, tile, line],
        in_specs=[hbm] * 8,
        out_specs=[vmem] * 4,
        scratch_shapes=[
            pltpu.SMEM(manning_table.shape, jnp.float32),
            pltpu.VMEM((4, rows, columns), jnp.float32),
            pltpu.VMEM((rows, columns), jnp.int32),
            pltpu.VMEM((4, 2 * HALO, columns), jnp.float32),
            pltpu.VMEM((2 * HALO, columns), jnp.int32),
            pltpu.VMEM((len(TIERS) - 1, 4, 2 * HALO, columns), jnp.float32),
            pltpu.VMEM((len(TIERS) - 1, 2 * HALO, columns), jnp.int32),
            pltpu.VMEM((STEPS - 1, TILE, columns), jnp.float32),
            pltpu.VMEM((STEPS - 1, TILE, columns), jnp.float32),
        ]
        + [wide] * 13
        + [
            tile,
            pltpu.VMEM((5, 1, owned), jnp.float32),
            pltpu.VMEM((5, width, owned), jnp.int32),
            pltpu.VMEM((3, 1, owned), jnp.float32),
            line,
            line,
            dma((8,)),
            dma((2, 15)),
            dma((2, 15)),
            dma((2, 4)),
            dma((2, 4)),
            dma((2,)),
            dma((2,)),
        ],
        compiler_params=pltpu.CompilerParams(
            collective_id=0, has_side_effects=True, vmem_limit_bytes=VMEM_BYTES
        ),
        name="flood",
    )(*operands)
    depth, flux_east, flux_south, section = finish(depth, flux_east, flux_south, section)
    return depth, flux_east, flux_south, section.reshape(owned)


def solution(mesh):
    return jax.shard_map(
        local,
        mesh=mesh,
        in_specs=(
            P(("runs", "gy"), None),
            P(("runs", "gy"), None),
            P(("runs", "gy"), None),
            P(("runs", "gy")),
            P("gy", None),
            P("gy", None),
            P(),
            P(None, "gy"),
        ),
        out_specs=(
            P(("runs", "gy"), None),
            P(("runs", "gy"), None),
            P(("runs", "gy"), None),
            P(("runs", "gy")),
        ),
        check_vma=False,
    )
```

```python
import math

import jax
import jax.numpy as jnp
from jax import lax
from jax.experimental import pallas as pl
from jax.experimental.pallas import tpu as pltpu
from jax.sharding import PartitionSpec as P

STEPS = 4
HALO = STEPS
TIERS = ((0, 2), (2, 3), (3, 4))
LANES = 128
TILE = 8

GRAV = 9.81
TSTEP = 8.0
CELL = 90.0
FLOOR = 0.05
BANK_COEF = 200.0
CELL_AREA = 8100.0
NODE_AREA = 20000.0

SLOPE = GRAV * TSTEP / CELL
LEVEL = SLOPE * TSTEP / CELL
FLOW = LEVEL * TSTEP / CELL
ROUGH = math.sqrt(0.25 * GRAV * TSTEP * LEVEL ** (7.0 / 3.0) / FLOW)
KEEP = 1.0 - TSTEP * BANK_COEF * 4.0 / NODE_AREA
GAIN = TSTEP * BANK_COEF / NODE_AREA
INTO = TSTEP * BANK_COEF / CELL_AREA

MESH = pl.DeviceIdType.MESH
VMEM_BYTES = 24 * 1024 * 1024
FAR = -(1 << 24)
OFFSETS = (-1, 1, -2, 2)


def wave(batches):
    running, waiting = [], list(batches)
    while running or waiting:
        if waiting:
            running.extend(waiting.pop(0))
        for unit in list(running):
            try:
                next(unit)
            except StopIteration:
                running.remove(unit)


def by(size, units):
    units = list(units)
    return [units[i : i + size] for i in range(0, len(units), size)]


def halves(value):
    high = value.astype(jnp.bfloat16)
    return high, (value - high.astype(jnp.float32)).astype(jnp.bfloat16)


def flood_kernel(
    table_in,
    depth_in,
    east_in,
    south_in,
    bed_in,
    rough_in,
    section_in,
    cells_in,
    depth_out,
    east_out,
    south_out,
    section_out,
    table,
    raw,
    raw_rough,
    edge,
    edge_rough,
    far,
    far_rough,
    tops,
    bottoms,
    surf,
    fe,
    fs,
    bed,
    mann,
    max_e,
    max_s,
    drag_e,
    drag_s,
    tally,
    number,
    number4,
    boxes,
    partial,
    sections,
    cells,
    part,
    low,
    high,
    in_sem,
    strip_ssem,
    strip_rsem,
    node_ssem,
    node_rsem,
    part_ssem,
    part_rsem,
):
    me = lax.axis_index("gy")
    tiles = lax.axis_size("gy")
    rows, columns = depth_in.shape
    ext = rows + 2 * HALO
    chunks = columns // LANES
    owned = section_in.shape[1]
    total = 5 * owned

    def there(offset):
        return (me + offset >= 0) & (me + offset < tiles)

    def absent(offset):
        return jnp.logical_not(there(offset))

    edge[...] = jnp.zeros(edge.shape, jnp.float32)
    edge_rough[...] = jnp.zeros(edge_rough.shape, jnp.int32)
    barrier = pltpu.get_barrier_semaphore()
    for offset in OFFSETS:
        @pl.when(there(offset))
        def _():
            pl.semaphore_signal(
                barrier, inc=1, device_id={"gy": me + offset}, device_id_type=MESH
            )

    fields = (depth_in, bed_in, east_in, south_in)
    loads = [
        pltpu.make_async_copy(source, target, in_sem.at[i])
        for i, (source, target) in enumerate(
            [(field, raw.at[i]) for i, field in enumerate(fields)]
            + [
                (rough_in, raw_rough),
                (table_in, table),
                (section_in, sections.at[2]),
                (cells_in, cells.at[2]),
            ]
        )
    ]
    for load in loads:
        load.start()

    def send(src, dst, ssem, rsem, offset):
        return pltpu.make_async_remote_copy(
            src_ref=src,
            dst_ref=dst,
            send_sem=ssem,
            recv_sem=rsem,
            device_id={"gy": me + offset},
            device_id_type=MESH,
        )

    node_sends = {}
    for i, offset in enumerate(OFFSETS):
        slot = 2 - offset
        node_sends[offset] = (
            send(section_in, sections.at[slot], node_ssem.at[0, i], node_rsem.at[0, i], offset),
            send(cells_in, cells.at[slot], node_ssem.at[1, i], node_rsem.at[1, i], offset),
        )
    def span_of(tier, field, offset):
        first, stop = TIERS[tier]
        if field == 2 or (field == 3 and offset < 0):
            return max(first - 1, 0), stop - 1
        return first, stop

    def landing(tier, field, offset):
        first, stop = span_of(tier, field, offset)
        return slice(first, stop) if offset < 0 else slice(2 * HALO - stop, 2 * HALO - first)

    strip_sends = {}
    for i, offset in enumerate((-1, 1)):
        for tier in range(len(TIERS)):
            strip_sends[tier, offset] = []
            for j in range(5):
                first, stop = span_of(tier, j, offset)
                theirs = slice(first, stop) if offset < 0 else slice(rows - stop, rows - first)
                lands = landing(tier, j, offset)
                if j < 4:
                    source = fields[j].at[theirs]
                    target = edge.at[j, lands] if tier == 0 else far.at[tier - 1, j, lands]
                else:
                    source = rough_in.at[theirs]
                    target = edge_rough.at[lands] if tier == 0 else far_rough.at[tier - 1, lands]
                sem = 5 * tier + j
                strip_sends[tier, offset].append(
                    send(source, target, strip_ssem.at[i, sem], strip_rsem.at[i, sem], offset)
                )

    pl.semaphore_wait(barrier, jnp.minimum(me, 2) + jnp.minimum(tiles - 1 - me, 2))
    for offset in OFFSETS:
        @pl.when(there(offset))
        def _():
            for copy in node_sends[offset]:
                copy.start()

    for tier in range(len(TIERS)):
        for offset in (-1, 1):
            @pl.when(there(offset))
            def _():
                for copy in strip_sends[tier, offset]:
                    copy.start()

    for load in loads:
        load.wait()

    scaled = [table[k] * ROUGH for k in range(table.shape[0])]

    def roughness(rough):
        values, bit = scaled, 1
        while len(values) > 1:
            odd = (rough & bit) != 0
            values = [
                jnp.where(odd, values[i + 1], values[i]) if i + 1 < len(values) else values[i]
                for i in range(0, len(values), 2)
            ]
            bit *= 2
        return values[0]

    def at(c):
        return slice(LANES * c, LANES * (c + 1))

    lane_id = lax.broadcasted_iota(jnp.int32, (1, LANES), 1)

    def turn(value, shift):
        return pltpu.roll(value, LANES - shift, 1)

    def lanes_to(value, preceding, shift):
        mixed = jnp.where(lane_id < LANES - shift, value, preceding)
        return pltpu.roll(mixed, shift, 1)

    def south(value):
        return pltpu.roll(value, value.shape[0] - 1, 0)

    def north(value):
        return pltpu.roll(value, 1, 0)

    row_id = lax.broadcasted_iota(jnp.int32, (TILE, LANES), 0)
    shut_last = (row_id == TILE - 1) & (me == tiles - 1)
    shut_first = (row_id == TILE - 1) & (me == 0)

    def depth_of(surf_a, surf_b, bed_top):
        return jnp.maximum(jnp.maximum(surf_a, surf_b) - bed_top, FLOOR * LEVEL)

    def power_log(flow_depth):
        return lax.log2(flow_depth) * (-7.0 / 3.0)

    def damping(flux, drag, power):
        return 1.0 / (1.0 + drag * jnp.abs(flux) * power)

    def square(value):
        return value * value

    def closed_east(c, flux):
        return jnp.where(lane_id == LANES - 1, 0.0, flux) if c == chunks - 1 else flux

    def closed_south(flux):
        count = flux.shape[0]
        return jnp.concatenate(
            [flux[: count - 2 * TILE]] * (count > 2 * TILE)
            + [
                jnp.where(shut_last, 0.0, flux[count - 2 * TILE : count - TILE]),
                jnp.where(shut_first, 0.0, flux[count - TILE :]),
            ],
            axis=0,
        )

    def last_four(value, carried):
        pair = value + lanes_to(value, carried[0], 1)
        return pair + lanes_to(pair, carried[1], 2), (value, pair)

    def zeros(count):
        return jnp.zeros((count, LANES), jnp.float32)

    after = {}

    def put(name, c, value):
        after[name, c] = value

    def got(name, c, count):
        return after.get((name, c), zeros(count))

    def two_on(name, c, count):
        return jnp.where(lane_id < LANES - 2, after[name, c], got(name, c + 1, count))

    inner = rows - TILE

    def own_chunk(c):
        floor = raw[1, :, at(c)] * LEVEL
        bed[:rows, at(c)] = floor
        mine = roughness(raw_rough[:, at(c)])
        mann[:rows, at(c)] = mine
        here = raw[0, :, at(c)] * LEVEL + floor
        surf[:rows, at(c)] = here
        tops[0, :, at(c)] = here[:TILE]
        turned = [turn(a, 1) for a in (here, floor, mine)]
        put("own", c, (here, turned))
        yield
        yield
        following = after.get(("own", c + 1), (zeros(rows), [zeros(rows)] * 3))
        east, floor_e, mann_e = (
            jnp.where(lane_id < LANES - 1, a, b) for a, b in zip(turned, following[1])
        )
        pair = here + east
        put("pair", c, turn(pair, 2))
        top = jnp.maximum(floor, floor_e)
        drag = square(mine + mann_e)
        max_e[:rows, at(c)] = top
        drag_e[:rows, at(c)] = drag
        depth_e = depth_of(here, east, top)
        log_e = power_log(depth_e)
        below_s = south(here)[:inner]
        top = jnp.maximum(floor, south(floor))[:inner]
        drag_b = square((mine + south(mine))[:inner])
        max_s[:inner, at(c)] = top
        drag_s[:inner, at(c)] = drag_b
        depth_s = depth_of(here[:inner], below_s, top)
        log_s = power_log(depth_s)
        yield
        power_e, power_s = jnp.exp2(log_e), jnp.exp2(log_s)
        flux_e = raw[2, :, at(c)] * FLOW
        flux_s = raw[3, :inner, at(c)] * FLOW
        yield
        boxes[:rows, at(c)] = pair + two_on("pair", c, rows)
        damp_e = damping(flux_e, drag, power_e)
        damp_s = damping(flux_s, drag_b, power_s)
        yield
        new_east = closed_east(c, (flux_e - depth_e * (east - here)) * damp_e)
        new_south = (flux_s - depth_s * (below_s - here[:inner])) * damp_s
        fe[:rows, at(c)] = new_east
        fs[:inner, at(c)] = new_south
        put("east", c, new_east)
        west = lanes_to(new_east, got("east", c - 1, rows), 1)
        yield
        partial[:, at(c)] = here + (west - new_east)

    wave(by(2, (own_chunk(c) for c in range(chunks))))
    after.clear()

    def nodes_of(offsets):
        for offset in offsets:
            @pl.when(there(-offset))
            def _():
                for copy in node_sends[offset]:
                    copy.wait_recv()

            @pl.when(absent(-offset))
            def _():
                sections[2 - offset] = jnp.zeros((1, owned), jnp.float32)
                cells[2 - offset] = jnp.full((cells.shape[1], owned), FAR, jnp.int32)

    def one_hot(count, index):
        found = lax.broadcasted_iota(jnp.int32, (count, index.shape[1]), 0) == index
        return jnp.where(found, 1.0, 0.0).astype(jnp.bfloat16)

    def locate(slots):
        section = jnp.concatenate([sections[i] for i in slots], axis=1)
        cell = jnp.concatenate([cells[i, 0:1, :] for i in slots], axis=1)
        local = cell - (me * rows - HALO) * columns
        valid = (local >= 0) & (local < ext * columns)
        local = jnp.where(valid, local, 0)
        from_top = ((local.astype(jnp.float32) + 0.5) * (1.0 / columns)).astype(jnp.int32)
        column = local - from_top * columns
        chunk = column >> 7
        own = valid & (from_top >= HALO) & (from_top < rows + HALO)
        place = jnp.where(own, chunk * rows + from_top - HALO, -1)
        beyond = jnp.where(from_top < HALO, from_top + HALO, from_top - rows - HALO)
        place_edge = jnp.where(valid & jnp.logical_not(own), chunk * TILE + beyond, -1)
        lane = column & (LANES - 1)
        lane_hit = lax.broadcasted_iota(jnp.int32, (LANES, lane.shape[1]), 0) == lane
        levels = section * (LEVEL * INTO)
        level_high = levels.astype(jnp.bfloat16).astype(jnp.float32)
        weights = jnp.concatenate(
            [
                jnp.where(lane_hit, value, 0.0)
                for value in (level_high, levels - level_high, jnp.ones_like(levels))
            ],
            axis=0,
        ).astype(jnp.bfloat16)
        return section, own, place, place_edge, lane_hit, weights

    def spread_by(hits, weights):
        return lax.dot_general(
            hits, weights, (((1,), (1,)), ((), ())), preferred_element_type=jnp.float32
        )

    def planes(block):
        level = block[:, :LANES] + block[:, LANES : 2 * LANES]
        return level, block[:, 2 * LANES :] * INTO

    def share(name, span, c, level, count):
        count4, counted[name] = last_four(count, counted[name])
        tally[span, at(c)] = level
        number[span, at(c)] = count * GAIN
        number4[span, at(c)] = count4

    outer = slice(rows, ext)
    counted = {"own": (zeros(rows),) * 2, "edge": (zeros(TILE),) * 2}
    section_m, own_m, place, place_m, lane_m, weights_m = locate((2,))
    hit_m = one_hot(chunks * rows, place)
    spread = spread_by(hit_m, weights_m)
    for c in range(chunks):
        level, count = planes(spread[c * rows : (c + 1) * rows])
        tally[:rows, at(c)] = level
        number[:rows, at(c)] = count
    nodes_of((-1, 1))
    section_n, own_n, place, place_n, lane_n, weights_n = locate((1, 3))
    hit_n = one_hot(chunks * rows, place)
    spread = spread_by(hit_n, weights_n)
    for c in range(chunks):
        level, count = planes(spread[c * rows : (c + 1) * rows])
        level = level + tally[:rows, at(c)]
        share("own", slice(0, rows), c, level, count + number[:rows, at(c)])

    for offset in (-1, 1):
        @pl.when(there(-offset))
        def _():
            for copy in strip_sends[0, offset]:
                copy.wait_recv()

    def edge_chunk(c):
        floor = edge[1, :, at(c)] * LEVEL
        here = edge[0, :, at(c)] * LEVEL + floor
        mine = roughness(edge_rough[:, at(c)])
        turned = [turn(a, 1) for a in (here, floor, mine)]
        put("edge", c, (here, turned))
        yield
        yield
        following = after.get(("edge", c + 1), (zeros(TILE), [zeros(TILE)] * 3))
        east, floor_e, mann_e = (
            jnp.where(lane_id < LANES - 1, a, b) for a, b in zip(turned, following[1])
        )
        top = jnp.maximum(floor, floor_e)
        drag = square(mine + mann_e)
        max_e[outer, at(c)] = top
        drag_e[outer, at(c)] = drag
        depth_e = depth_of(here, east, top)
        log_e = power_log(depth_e)
        whole = jnp.concatenate([surf[:rows, at(c)], here], axis=0)
        below_s = south(whole)[inner:]
        floor = jnp.concatenate([bed[:rows, at(c)], floor], axis=0)
        mine = jnp.concatenate([mann[:rows, at(c)], mine], axis=0)
        top = jnp.maximum(floor, south(floor))[inner:]
        drag_b = square((mine + south(mine))[inner:])
        max_s[inner:, at(c)] = top
        drag_s[inner:, at(c)] = drag_b
        depth_s = depth_of(whole[inner:], below_s, top)
        log_s = power_log(depth_s)
        levels = tally[:rows, at(c)]
        put("edge_levels", c, levels)
        spill = levels + lanes_to(levels, got("edge_levels", c - 1, rows), 1)
        put("edge_spill", c, spill)
        yield
        spill2 = lanes_to(spill, got("edge_spill", c - 1, rows), 2)
        power_e, power_s = jnp.exp2(log_e), jnp.exp2(log_s)
        flux_e = edge[2, :, at(c)] * FLOW
        flux_s = jnp.concatenate([raw[3, inner:, at(c)], edge[3, :, at(c)]], axis=0) * FLOW
        yield
        damp_e = damping(flux_e, drag, power_e)
        damp_s = damping(flux_s, drag_b, power_s)
        yield
        new_east = closed_east(c, (flux_e - depth_e * (east - here)) * damp_e)
        new_south = closed_south((flux_s - depth_s * (below_s - whole[inner:])) * damp_s)
        fe[outer, at(c)] = new_east
        fs[inner:, at(c)] = new_south
        bottoms[0, :, at(c)] = new_south[:TILE]
        put("edge_east", c, new_east)
        west = lanes_to(new_east, got("edge_east", c - 1, TILE), 1)
        new_south = jnp.concatenate([fs[:inner, at(c)], new_south], axis=0)
        yield
        gain_s = north(new_south) - new_south
        surf[:rows, at(c)] = (
            partial[:, at(c)]
            + gain_s[:rows]
            + (spill + spill2 - number4[:rows, at(c)] * whole[:rows])
        )
        surf[outer, at(c)] = here + (west - new_east) + gain_s[rows:]

    def edge_source(c):
        spill = spilled("edge_moved", c, tally[outer, at(c)])
        yield
        source = spill()
        yield
        here = (edge[0, :, at(c)] + edge[1, :, at(c)]) * LEVEL
        surf[outer, at(c)] = surf[outer, at(c)] + (source - number4[outer, at(c)] * here)

    def spilled(name, c, moved):
        count = moved.shape[0]
        put((name, 1), c, moved)
        once = moved + lanes_to(moved, got((name, 1), c - 1, count), 1)
        put((name, 2), c, once)
        return lambda: once + lanes_to(once, got((name, 2), c - 1, count), 2)

    def chunk_step(step, c):
        count = rows
        span = slice(0, count)
        whole = surf[:, at(c)]
        here = whole[:count]
        tops[step, :, at(c)] = whole[:TILE]
        turned = turn(here, 1)
        put(("here", step), c, (here, turned))
        yield
        yield
        following = after.get((("here", step), c + 1), (zeros(count), zeros(count)))
        east = jnp.where(lane_id < LANES - 1, turned, following[1])
        depth_e = depth_of(here, east, max_e[span, at(c)])
        log_e = power_log(depth_e)
        below_s = south(whole)
        depth_s = depth_of(whole, below_s, max_s[:, at(c)])
        log_s = power_log(depth_s)
        pair = here + east
        put(("pair", step), c, turn(pair, 2))
        box = boxes[span, at(c)]
        spill = spilled(("moved", step), c, number[span, at(c)] * box + KEEP**step * tally[span, at(c)])
        yield
        power_e, power_s = jnp.exp2(log_e), jnp.exp2(log_s)
        source = spill()
        yield
        boxes[span, at(c)] = KEEP * box + (pair + two_on(("pair", step), c, count))
        flux_e, flux_s = fe[span, at(c)], fs[:, at(c)]
        damp_e = damping(flux_e, drag_e[span, at(c)], power_e)
        damp_s = damping(flux_s, drag_s[:, at(c)], power_s)
        source = source - number4[span, at(c)] * here
        yield
        new_east = closed_east(c, (flux_e - depth_e * (east - here)) * damp_e)
        new_south = closed_south((flux_s - depth_s * (below_s - whole)) * damp_s)
        put(("east", step), c, new_east)
        west = lanes_to(new_east, got(("east", step), c - 1, count), 1)
        fe[span, at(c)] = new_east
        fs[span, at(c)] = new_south[:count]
        bottoms[step, :, at(c)] = new_south[inner:rows]
        yield
        level = here + (west - new_east) + (north(new_south) - new_south)[:count] + source
        surf[span, at(c)] = level

    def halo_step(step, c):
        if step == 0:
            floor = edge[1, :, at(c)] * LEVEL
            here = edge[0, :, at(c)] * LEVEL + floor
            mine = roughness(edge_rough[:, at(c)])
            turned = [turn(a, 1) for a in (here, floor, mine)]
        else:
            here = surf[outer, at(c)]
            turned = [turn(here, 1)]
        put(("halo", step), c, turned)
        yield
        yield
        following = after.get((("halo", step), c + 1), [zeros(TILE)] * 3)
        nexts = [jnp.where(lane_id < LANES - 1, a, b) for a, b in zip(turned, following)]
        east = nexts[0]
        pair = here + east
        put(("halo_pair", step), c, turn(pair, 2))

        def southward(value, top):
            return south(jnp.concatenate([value, top], axis=0))[:TILE]

        below_s = southward(here, tops[step, :, at(c)])
        if step == 0:
            top = jnp.maximum(floor, nexts[1])
            drag = square(mine + nexts[2])
            top_s = jnp.maximum(floor, southward(floor, bed[:TILE, at(c)]))
            drag_b = square(mine + southward(mine, mann[:TILE, at(c)]))
            max_e[outer, at(c)] = top
            drag_e[outer, at(c)] = drag
            max_s[outer, at(c)] = top_s
            drag_s[outer, at(c)] = drag_b
            flux_e, flux_s = (edge[i, :, at(c)] * FLOW for i in (2, 3))
            moved = tally[outer, at(c)]
        else:
            top, drag = max_e[outer, at(c)], drag_e[outer, at(c)]
            top_s, drag_b = max_s[outer, at(c)], drag_s[outer, at(c)]
            flux_e, flux_s = fe[outer, at(c)], fs[outer, at(c)]
            box = boxes[outer, at(c)]
            moved = number[outer, at(c)] * box + KEEP**step * tally[outer, at(c)]
        depth_e = depth_of(here, east, top)
        log_e = power_log(depth_e)
        depth_s = depth_of(here, below_s, top_s)
        log_s = power_log(depth_s)
        spill = spilled(("halo_moved", step), c, moved)
        yield
        power_e, power_s = jnp.exp2(log_e), jnp.exp2(log_s)
        source = spill()
        yield
        total = pair + two_on(("halo_pair", step), c, TILE)
        boxes[outer, at(c)] = total if step == 0 else KEEP * box + total
        damp_e = damping(flux_e, drag, power_e)
        damp_s = damping(flux_s, drag_b, power_s)
        source = source - number4[outer, at(c)] * here
        yield
        new_east = closed_east(c, (flux_e - depth_e * (east - here)) * damp_e)
        new_south = (flux_s - depth_s * (below_s - here)) * damp_s
        new_south = jnp.where(shut_first, 0.0, new_south)
        put(("halo_east", step), c, new_east)
        west = lanes_to(new_east, got(("halo_east", step), c - 1, TILE), 1)
        fe[outer, at(c)] = new_east
        fs[outer, at(c)] = new_south
        yield
        into = north(jnp.concatenate([bottoms[step, :, at(c)], new_south], axis=0))[TILE:]
        surf[outer, at(c)] = here + (west - new_east) + (into - new_south) + source

    def part_chunk(step, c):
        last = step == STEPS - 1
        here = surf[:rows, at(c)]
        turned = turn(here, 1)
        put(("here", step), c, (here, turned))
        if not last:
            tops[step, :, at(c)] = here[:TILE]
        yield
        yield
        following = after.get((("here", step), c + 1), (zeros(rows), zeros(rows)))
        east = jnp.where(lane_id < LANES - 1, turned, following[1])
        depth_e = depth_of(here, east, max_e[:rows, at(c)])
        log_e = power_log(depth_e)
        below_s = south(here)[:inner]
        depth_s = depth_of(here[:inner], below_s, max_s[:inner, at(c)])
        log_s = power_log(depth_s)
        if not last:
            pair = here + east
            put(("pair", step), c, turn(pair, 2))
        box = boxes[:rows, at(c)]
        spill = spilled(
            ("moved", step), c, number[:rows, at(c)] * box + KEEP**step * tally[:rows, at(c)]
        )
        yield
        power_e, power_s = jnp.exp2(log_e), jnp.exp2(log_s)
        source = spill()
        yield
        if not last:
            boxes[:rows, at(c)] = KEEP * box + (pair + two_on(("pair", step), c, rows))
        flux_e, flux_s = fe[:rows, at(c)], fs[:inner, at(c)]
        damp_e = damping(flux_e, drag_e[:rows, at(c)], power_e)
        damp_s = damping(flux_s, drag_s[:inner, at(c)], power_s)
        source = source - number4[:rows, at(c)] * here
        yield
        new_east = closed_east(c, (flux_e - depth_e * (east - here)) * damp_e)
        new_south = (flux_s - depth_s * (below_s - here[:inner])) * damp_s
        put(("east", step), c, new_east)
        west = lanes_to(new_east, got(("east", step), c - 1, rows), 1)
        fs[:inner, at(c)] = new_south
        if last:
            east_out[:, at(c)] = new_east * (1.0 / FLOW)
            south_out[:inner, at(c)] = new_south * (1.0 / FLOW)
        else:
            fe[:rows, at(c)] = new_east
        yield
        partial[:, at(c)] = here + (west - new_east) + source

    def join_chunk(step, c):
        last = step == STEPS - 1
        whole = jnp.concatenate([surf[inner:, at(c)], surf[:TILE, at(c)]], axis=0)
        here = whole[: 2 * TILE]
        below_s = south(whole)[: 2 * TILE]
        depth_s = depth_of(here, below_s, max_s[inner:, at(c)])
        log_s = power_log(depth_s)
        yield
        power_s = jnp.exp2(log_s)
        flux_s = fs[inner:, at(c)]
        yield
        damp_s = damping(flux_s, drag_s[inner:, at(c)], power_s)
        yield
        new_south = closed_south((flux_s - depth_s * (below_s - here)) * damp_s)
        if last:
            south_out[inner:, at(c)] = new_south[:TILE] * (1.0 / FLOW)
        else:
            fs[inner:rows, at(c)] = new_south[:TILE]
            bottoms[step, :, at(c)] = new_south[:TILE]
        new_south = jnp.concatenate([fs[:inner, at(c)], new_south], axis=0)
        level = partial[:, at(c)] + (north(new_south) - new_south)[:rows]
        if last:
            depth_out[:, at(c)] = level * (1.0 / LEVEL) - raw[1, :, at(c)]
        else:
            surf[:rows, at(c)] = level

    def arrive(tier):
        for offset in (-1, 1):
            @pl.when(there(-offset))
            def _():
                for copy in strip_sends[tier, offset]:
                    copy.wait_recv()

                for j in range(4):
                    lands = landing(tier, j, offset)
                    edge[j, lands, :] = far[tier - 1, j, lands, :]
                lands = landing(tier, 4, offset)
                edge_rough[lands, :] = far_rough[tier - 1, lands, :]

    def again(steps, step, extra):
        batches = []
        for done in range(steps):
            batches += by(5, (halo_step(done, c) for c in range(chunks))) + [[]] * 4
        for i, batch in enumerate(by(5, (part_chunk(step, c) for c in range(chunks)))):
            batches[i + 3] = batches[i + 3] + batch
        wave(batches + by(5, (join_chunk(step, c) for c in range(chunks))) + extra)

    flat = {}

    def node_chunk(c):
        here = surf[:rows, at(c)]
        turned = turn(here, 1)
        put("node", c, (here, turned))
        yield
        yield
        following = after.get(("node", c + 1), (zeros(rows), zeros(rows)))
        pair = here + jnp.where(lane_id < LANES - 1, turned, following[1])
        put("node_pair", c, turn(pair, 2))
        yield
        yield
        flat[c] = KEEP * boxes[:rows, at(c)] + (pair + two_on("node_pair", c, rows))

    wave(by(15, (edge_chunk(c) for c in range(chunks))))

    nodes_of((-2, 2))
    _, _, _, place_f, _, weights_f = locate((0, 4))
    hit_edge = one_hot(
        -(-chunks * TILE // 16) * 16, jnp.concatenate([place_m, place_n, place_f], axis=1)
    )
    spread = spread_by(hit_edge, jnp.concatenate([weights_m, weights_n, weights_f], axis=1))
    for c in range(chunks):
        share("edge", outer, c, *planes(spread[c * TILE : (c + 1) * TILE]))
    wave(by(5, (edge_source(c) for c in range(chunks))) + [[]] + by(4, (chunk_step(1, c) for c in range(chunks))))

    arrive(1)
    again(2, 2, by(5, (node_chunk(c) for c in range(chunks))))
    flat = [flat[c] for c in range(chunks)]

    turned = jnp.concatenate(halves(jnp.concatenate(flat, axis=0).T), axis=0)

    def levels_of(section, own, hit, lane_hit):
        picked = jnp.dot(turned, hit, preferred_element_type=jnp.float32)
        picked = picked[:LANES] + picked[LANES:]
        picked = jnp.sum(jnp.where(lane_hit, picked, 0.0), axis=0, keepdims=True)
        return jnp.where(own, KEEP**STEPS * section + (GAIN / LEVEL) * picked, 0.0)

    final = levels_of(section_n, own_n, hit_n, lane_n)
    part[0] = final[:, :owned]
    part[2] = final[:, owned:]

    part_prev = send(part.at[0], high, part_ssem.at[0], part_rsem.at[0], -1)
    part_next = send(part.at[2], low, part_ssem.at[1], part_rsem.at[1], 1)

    @pl.when(there(-1))
    def _():
        part_prev.start()

    @pl.when(there(1))
    def _():
        part_next.start()

    part[1] = levels_of(section_m, own_m, hit_m, lane_m)

    arrive(2)
    again(3, 3, [])

    for offset in OFFSETS:
        @pl.when(there(offset))
        def _():
            for copy in node_sends[offset]:
                copy.wait_send()

    for offset in (-1, 1):
        @pl.when(there(offset))
        def _():
            for tier in range(len(TIERS)):
                for copy in strip_sends[tier, offset]:
                    copy.wait_send()

    section_out[...] = part[1]

    @pl.when(there(1))
    def _():
        part_prev.wait_recv()
        section_out[...] += high[...]

    @pl.when(there(-1))
    def _():
        part_next.wait_recv()
        section_out[...] += low[...]

    @pl.when(there(-1))
    def _():
        part_prev.wait_send()

    @pl.when(there(1))
    def _():
        part_next.wait_send()


def finish_kernel(a, b, c, d, a_out, b_out, c_out, d_out, out_sem):
    stores = [
        pltpu.make_async_copy(source, target, out_sem.at[i])
        for i, (source, target) in enumerate(
            ((a, a_out), (b, b_out), (c, c_out), (d, d_out))
        )
    ]
    for store in stores:
        store.start()
    for store in stores:
        store.wait()


def finish(*arrays):
    return pl.pallas_call(
        finish_kernel,
        out_shape=[jax.ShapeDtypeStruct(a.shape, a.dtype) for a in arrays],
        in_specs=[pl.BlockSpec(memory_space=pltpu.VMEM)] * 4,
        out_specs=[pl.BlockSpec(memory_space=pltpu.MemorySpace.HBM)] * 4,
        scratch_shapes=[pltpu.SemaphoreType.DMA((4,))],
        compiler_params=pltpu.CompilerParams(vmem_limit_bytes=VMEM_BYTES),
        name="finish",
    )(*arrays)


def local(
    depth, flux_east, flux_south, river_section, bed_level, rough_class, manning_table, bank_cell
):
    rows, columns = depth.shape
    owned = river_section.shape[0]
    width, _ = bank_cell.shape
    ext = rows + 2 * HALO
    operands = [
        pltpu.with_memory_space_constraint(a, pltpu.MemorySpace.HBM)
        for a in (
            manning_table,
            depth,
            flux_east,
            flux_south,
            bed_level,
            rough_class,
            river_section.reshape(1, owned),
            bank_cell,
        )
    ]
    hbm = pl.BlockSpec(memory_space=pltpu.MemorySpace.HBM)
    vmem = pl.BlockSpec(memory_space=pltpu.VMEM)
    tile = pltpu.VMEM((rows, columns), jnp.float32)
    line = pltpu.VMEM((1, owned), jnp.float32)
    wide = pltpu.VMEM((ext, columns), jnp.float32)
    dma = pltpu.SemaphoreType.DMA
    depth, flux_east, flux_south, section = pl.pallas_call(
        flood_kernel,
        out_shape=[tile, tile, tile, line],
        in_specs=[hbm] * 8,
        out_specs=[vmem] * 4,
        scratch_shapes=[
            pltpu.SMEM(manning_table.shape, jnp.float32),
            pltpu.VMEM((4, rows, columns), jnp.float32),
            pltpu.VMEM((rows, columns), jnp.int32),
            pltpu.VMEM((4, 2 * HALO, columns), jnp.float32),
            pltpu.VMEM((2 * HALO, columns), jnp.int32),
            pltpu.VMEM((len(TIERS) - 1, 4, 2 * HALO, columns), jnp.float32),
            pltpu.VMEM((len(TIERS) - 1, 2 * HALO, columns), jnp.int32),
            pltpu.VMEM((STEPS - 1, TILE, columns), jnp.float32),
            pltpu.VMEM((STEPS - 1, TILE, columns), jnp.float32),
        ]
        + [wide] * 13
        + [
            tile,
            pltpu.VMEM((5, 1, owned), jnp.float32),
            pltpu.VMEM((5, width, owned), jnp.int32),
            pltpu.VMEM((3, 1, owned), jnp.float32),
            line,
            line,
            dma((8,)),
            dma((2, 15)),
            dma((2, 15)),
            dma((2, 4)),
            dma((2, 4)),
            dma((2,)),
            dma((2,)),
        ],
        compiler_params=pltpu.CompilerParams(
            collective_id=0, has_side_effects=True, vmem_limit_bytes=VMEM_BYTES
        ),
        name="flood",
    )(*operands)
    depth, flux_east, flux_south, section = finish(depth, flux_east, flux_south, section)
    return depth, flux_east, flux_south, section.reshape(owned)


def solution(mesh):
    return jax.shard_map(
        local,
        mesh=mesh,
        in_specs=(
            P(("runs", "gy"), None),
            P(("runs", "gy"), None),
            P(("runs", "gy"), None),
            P(("runs", "gy")),
            P("gy", None),
            P("gy", None),
            P(),
            P(None, "gy"),
        ),
        out_specs=(
            P(("runs", "gy"), None),
            P(("runs", "gy"), None),
            P(("runs", "gy"), None),
            P(("runs", "gy")),
        ),
        check_vma=False,
    )
```

```python
import math

import jax
import jax.numpy as jnp
from jax import lax
from jax.experimental import pallas as pl
from jax.experimental.pallas import tpu as pltpu
from jax.sharding import PartitionSpec as P

STEPS = 4
HALO = STEPS
TIERS = ((0, 2), (2, 3), (3, 4))
LANES = 128
TILE = 8

GRAV = 9.81
TSTEP = 8.0
CELL = 90.0
FLOOR = 0.05
BANK_COEF = 200.0
CELL_AREA = 8100.0
NODE_AREA = 20000.0

SLOPE = GRAV * TSTEP / CELL
LEVEL = SLOPE * TSTEP / CELL
FLOW = LEVEL * TSTEP / CELL
ROUGH = math.sqrt(0.25 * GRAV * TSTEP * LEVEL ** (7.0 / 3.0) / FLOW)
KEEP = 1.0 - TSTEP * BANK_COEF * 4.0 / NODE_AREA
GAIN = TSTEP * BANK_COEF / NODE_AREA
INTO = TSTEP * BANK_COEF / CELL_AREA

MESH = pl.DeviceIdType.MESH
VMEM_BYTES = 24 * 1024 * 1024
FAR = -(1 << 24)
OFFSETS = (-1, 1, -2, 2)


def wave(batches):
    running, waiting = [], list(batches)
    while running or waiting:
        if waiting:
            running.extend(waiting.pop(0))
        for unit in list(running):
            try:
                next(unit)
            except StopIteration:
                running.remove(unit)


def by(size, units):
    units = list(units)
    return [units[i : i + size] for i in range(0, len(units), size)]


def halves(value):
    high = value.astype(jnp.bfloat16)
    return high, (value - high.astype(jnp.float32)).astype(jnp.bfloat16)


def flood_kernel(
    table_in,
    depth_in,
    east_in,
    south_in,
    bed_in,
    rough_in,
    section_in,
    cells_in,
    depth_out,
    east_out,
    south_out,
    section_out,
    table,
    raw,
    raw_rough,
    edge,
    edge_rough,
    far,
    far_rough,
    tops,
    bottoms,
    surf,
    fe,
    fs,
    bed,
    mann,
    max_e,
    max_s,
    drag_e,
    drag_s,
    tally,
    number,
    number4,
    boxes,
    partial,
    sections,
    cells,
    part,
    low,
    high,
    in_sem,
    strip_ssem,
    strip_rsem,
    node_ssem,
    node_rsem,
    part_ssem,
    part_rsem,
):
    me = lax.axis_index("gy")
    tiles = lax.axis_size("gy")
    rows, columns = depth_in.shape
    ext = rows + 2 * HALO
    chunks = columns // LANES
    owned = section_in.shape[1]
    total = 5 * owned

    def there(offset):
        return (me + offset >= 0) & (me + offset < tiles)

    def absent(offset):
        return jnp.logical_not(there(offset))

    edge[...] = jnp.zeros(edge.shape, jnp.float32)
    edge_rough[...] = jnp.zeros(edge_rough.shape, jnp.int32)
    barrier = pltpu.get_barrier_semaphore()
    for offset in OFFSETS:
        @pl.when(there(offset))
        def _():
            pl.semaphore_signal(
                barrier, inc=1, device_id={"gy": me + offset}, device_id_type=MESH
            )

    fields = (depth_in, bed_in, east_in, south_in)
    loads = [
        pltpu.make_async_copy(source, target, in_sem.at[i])
        for i, (source, target) in enumerate(
            [(field, raw.at[i]) for i, field in enumerate(fields)]
            + [
                (rough_in, raw_rough),
                (table_in, table),
                (section_in, sections.at[2]),
                (cells_in, cells.at[2]),
            ]
        )
    ]
    for load in loads:
        load.start()

    def send(src, dst, ssem, rsem, offset):
        return pltpu.make_async_remote_copy(
            src_ref=src,
            dst_ref=dst,
            send_sem=ssem,
            recv_sem=rsem,
            device_id={"gy": me + offset},
            device_id_type=MESH,
        )

    node_sends = {}
    for i, offset in enumerate(OFFSETS):
        slot = 2 - offset
        node_sends[offset] = (
            send(section_in, sections.at[slot], node_ssem.at[0, i], node_rsem.at[0, i], offset),
            send(cells_in, cells.at[slot], node_ssem.at[1, i], node_rsem.at[1, i], offset),
        )
    def span_of(tier, field, offset):
        first, stop = TIERS[tier]
        if field == 2 or (field == 3 and offset < 0):
            return max(first - 1, 0), stop - 1
        return first, stop

    def landing(tier, field, offset):
        first, stop = span_of(tier, field, offset)
        return slice(first, stop) if offset < 0 else slice(2 * HALO - stop, 2 * HALO - first)

    strip_sends = {}
    for i, offset in enumerate((-1, 1)):
        for tier in range(len(TIERS)):
            strip_sends[tier, offset] = []
            for j in range(5):
                first, stop = span_of(tier, j, offset)
                theirs = slice(first, stop) if offset < 0 else slice(rows - stop, rows - first)
                lands = landing(tier, j, offset)
                if j < 4:
                    source = fields[j].at[theirs]
                    target = edge.at[j, lands] if tier == 0 else far.at[tier - 1, j, lands]
                else:
                    source = rough_in.at[theirs]
                    target = edge_rough.at[lands] if tier == 0 else far_rough.at[tier - 1, lands]
                sem = 5 * tier + j
                strip_sends[tier, offset].append(
                    send(source, target, strip_ssem.at[i, sem], strip_rsem.at[i, sem], offset)
                )

    pl.semaphore_wait(barrier, jnp.minimum(me, 2) + jnp.minimum(tiles - 1 - me, 2))
    for offset in OFFSETS:
        @pl.when(there(offset))
        def _():
            for copy in node_sends[offset]:
                copy.start()

    for tier in range(len(TIERS)):
        for offset in (-1, 1):
            @pl.when(there(offset))
            def _():
                for copy in strip_sends[tier, offset]:
                    copy.start()

    for load in loads:
        load.wait()

    scaled = [table[k] * ROUGH for k in range(table.shape[0])]

    def roughness(rough):
        values, bit = scaled, 1
        while len(values) > 1:
            odd = (rough & bit) != 0
            values = [
                jnp.where(odd, values[i + 1], values[i]) if i + 1 < len(values) else values[i]
                for i in range(0, len(values), 2)
            ]
            bit *= 2
        return values[0]

    def at(c):
        return slice(LANES * c, LANES * (c + 1))

    lane_id = lax.broadcasted_iota(jnp.int32, (1, LANES), 1)

    def turn(value, shift):
        return pltpu.roll(value, LANES - shift, 1)

    def lanes_to(value, preceding, shift):
        mixed = jnp.where(lane_id < LANES - shift, value, preceding)
        return pltpu.roll(mixed, shift, 1)

    def south(value):
        return pltpu.roll(value, value.shape[0] - 1, 0)

    def north(value):
        return pltpu.roll(value, 1, 0)

    row_id = lax.broadcasted_iota(jnp.int32, (TILE, LANES), 0)
    shut_last = (row_id == TILE - 1) & (me == tiles - 1)
    shut_first = (row_id == TILE - 1) & (me == 0)

    def depth_of(surf_a, surf_b, bed_top):
        return jnp.maximum(jnp.maximum(surf_a, surf_b) - bed_top, FLOOR * LEVEL)

    def power_log(flow_depth):
        return lax.log2(flow_depth) * (-7.0 / 3.0)

    def damping(flux, drag, power):
        return 1.0 / (1.0 + drag * jnp.abs(flux) * power)

    def square(value):
        return value * value

    def closed_east(c, flux):
        return jnp.where(lane_id == LANES - 1, 0.0, flux) if c == chunks - 1 else flux

    def closed_south(flux):
        count = flux.shape[0]
        return jnp.concatenate(
            [flux[: count - 2 * TILE]] * (count > 2 * TILE)
            + [
                jnp.where(shut_last, 0.0, flux[count - 2 * TILE : count - TILE]),
                jnp.where(shut_first, 0.0, flux[count - TILE :]),
            ],
            axis=0,
        )

    def last_four(value, carried):
        pair = value + lanes_to(value, carried[0], 1)
        return pair + lanes_to(pair, carried[1], 2), (value, pair)

    def zeros(count):
        return jnp.zeros((count, LANES), jnp.float32)

    after = {}

    def put(name, c, value):
        after[name, c] = value

    def got(name, c, count):
        return after.get((name, c), zeros(count))

    def two_on(name, c, count):
        return jnp.where(lane_id < LANES - 2, after[name, c], got(name, c + 1, count))

    inner = rows - TILE

    def own_chunk(c):
        floor = raw[1, :, at(c)] * LEVEL
        bed[:rows, at(c)] = floor
        mine = roughness(raw_rough[:, at(c)])
        mann[:rows, at(c)] = mine
        here = raw[0, :, at(c)] * LEVEL + floor
        surf[:rows, at(c)] = here
        tops[0, :, at(c)] = here[:TILE]
        turned = [turn(a, 1) for a in (here, floor, mine)]
        put("own", c, (here, turned))
        yield
        yield
        following = after.get(("own", c + 1), (zeros(rows), [zeros(rows)] * 3))
        east, floor_e, mann_e = (
            jnp.where(lane_id < LANES - 1, a, b) for a, b in zip(turned, following[1])
        )
        pair = here + east
        put("pair", c, turn(pair, 2))
        top = jnp.maximum(floor, floor_e)
        drag = square(mine + mann_e)
        max_e[:rows, at(c)] = top
        drag_e[:rows, at(c)] = drag
        depth_e = depth_of(here, east, top)
        log_e = power_log(depth_e)
        below_s = south(here)[:inner]
        top = jnp.maximum(floor, south(floor))[:inner]
        drag_b = square((mine + south(mine))[:inner])
        max_s[:inner, at(c)] = top
        drag_s[:inner, at(c)] = drag_b
        depth_s = depth_of(here[:inner], below_s, top)
        log_s = power_log(depth_s)
        yield
        power_e, power_s = jnp.exp2(log_e), jnp.exp2(log_s)
        flux_e = raw[2, :, at(c)] * FLOW
        flux_s = raw[3, :inner, at(c)] * FLOW
        yield
        boxes[:rows, at(c)] = pair + two_on("pair", c, rows)
        damp_e = damping(flux_e, drag, power_e)
        damp_s = damping(flux_s, drag_b, power_s)
        yield
        new_east = closed_east(c, (flux_e - depth_e * (east - here)) * damp_e)
        new_south = (flux_s - depth_s * (below_s - here[:inner])) * damp_s
        fe[:rows, at(c)] = new_east
        fs[:inner, at(c)] = new_south
        put("east", c, new_east)
        west = lanes_to(new_east, got("east", c - 1, rows), 1)
        yield
        partial[:, at(c)] = here + (west - new_east)

    wave(by(2, (own_chunk(c) for c in range(chunks))))
    after.clear()

    def nodes_of(offsets):
        for offset in offsets:
            @pl.when(there(-offset))
            def _():
                for copy in node_sends[offset]:
                    copy.wait_recv()

            @pl.when(absent(-offset))
            def _():
                sections[2 - offset] = jnp.zeros((1, owned), jnp.float32)
                cells[2 - offset] = jnp.full((cells.shape[1], owned), FAR, jnp.int32)

    def one_hot(count, index):
        found = lax.broadcasted_iota(jnp.int32, (count, index.shape[1]), 0) == index
        return jnp.where(found, 1.0, 0.0).astype(jnp.bfloat16)

    def locate(slots):
        section = jnp.concatenate([sections[i] for i in slots], axis=1)
        cell = jnp.concatenate([cells[i, 0:1, :] for i in slots], axis=1)
        local = cell - (me * rows - HALO) * columns
        valid = (local >= 0) & (local < ext * columns)
        local = jnp.where(valid, local, 0)
        from_top = ((local.astype(jnp.float32) + 0.5) * (1.0 / columns)).astype(jnp.int32)
        column = local - from_top * columns
        chunk = column >> 7
        own = valid & (from_top >= HALO) & (from_top < rows + HALO)
        place = jnp.where(own, chunk * rows + from_top - HALO, -1)
        beyond = jnp.where(from_top < HALO, from_top + HALO, from_top - rows - HALO)
        place_edge = jnp.where(valid & jnp.logical_not(own), chunk * TILE + beyond, -1)
        lane = column & (LANES - 1)
        lane_hit = lax.broadcasted_iota(jnp.int32, (LANES, lane.shape[1]), 0) == lane
        levels = section * (LEVEL * INTO)
        level_high = levels.astype(jnp.bfloat16).astype(jnp.float32)
        weights = jnp.concatenate(
            [
                jnp.where(lane_hit, value, 0.0)
                for value in (level_high, levels - level_high, jnp.ones_like(levels))
            ],
            axis=0,
        ).astype(jnp.bfloat16)
        return section, own, place, place_edge, lane_hit, weights

    def spread_by(hits, weights):
        return lax.dot_general(
            hits, weights, (((1,), (1,)), ((), ())), preferred_element_type=jnp.float32
        )

    def planes(block):
        level = block[:, :LANES] + block[:, LANES : 2 * LANES]
        return level, block[:, 2 * LANES :] * INTO

    def share(name, span, c, level, count):
        count4, counted[name] = last_four(count, counted[name])
        tally[span, at(c)] = level
        number[span, at(c)] = count * GAIN
        number4[span, at(c)] = count4

    outer = slice(rows, ext)
    counted = {"own": (zeros(rows),) * 2, "edge": (zeros(TILE),) * 2}
    section_m, own_m, place, place_m, lane_m, weights_m = locate((2,))
    hit_m = one_hot(chunks * rows, place)
    spread = spread_by(hit_m, weights_m)
    for c in range(chunks):
        level, count = planes(spread[c * rows : (c + 1) * rows])
        tally[:rows, at(c)] = level
        number[:rows, at(c)] = count
    nodes_of((-1, 1))
    section_n, own_n, place, place_n, lane_n, weights_n = locate((1, 3))
    hit_n = one_hot(chunks * rows, place)
    spread = spread_by(hit_n, weights_n)
    for c in range(chunks):
        level, count = planes(spread[c * rows : (c + 1) * rows])
        level = level + tally[:rows, at(c)]
        share("own", slice(0, rows), c, level, count + number[:rows, at(c)])

    blocks = -(-chunks * TILE // 16) * 16
    spread = spread_by(
        one_hot(blocks, jnp.concatenate([place_m, place_n], axis=1)),
        jnp.concatenate([weights_m, weights_n], axis=1),
    )
    for c in range(chunks):
        level, count = planes(spread[c * TILE : (c + 1) * TILE])
        tally[outer, at(c)] = level
        number[outer, at(c)] = count

    for offset in (-1, 1):
        @pl.when(there(-offset))
        def _():
            for copy in strip_sends[0, offset]:
                copy.wait_recv()

    def edge_chunk(c):
        floor = edge[1, :, at(c)] * LEVEL
        here = edge[0, :, at(c)] * LEVEL + floor
        mine = roughness(edge_rough[:, at(c)])
        turned = [turn(a, 1) for a in (here, floor, mine)]
        put("edge", c, (here, turned))
        yield
        yield
        following = after.get(("edge", c + 1), (zeros(TILE), [zeros(TILE)] * 3))
        east, floor_e, mann_e = (
            jnp.where(lane_id < LANES - 1, a, b) for a, b in zip(turned, following[1])
        )
        top = jnp.maximum(floor, floor_e)
        drag = square(mine + mann_e)
        max_e[outer, at(c)] = top
        drag_e[outer, at(c)] = drag
        depth_e = depth_of(here, east, top)
        log_e = power_log(depth_e)
        whole = jnp.concatenate([surf[:rows, at(c)], here], axis=0)
        below_s = south(whole)[inner:]
        floor = jnp.concatenate([bed[:rows, at(c)], floor], axis=0)
        mine = jnp.concatenate([mann[:rows, at(c)], mine], axis=0)
        top = jnp.maximum(floor, south(floor))[inner:]
        drag_b = square((mine + south(mine))[inner:])
        max_s[inner:, at(c)] = top
        drag_s[inner:, at(c)] = drag_b
        depth_s = depth_of(whole[inner:], below_s, top)
        log_s = power_log(depth_s)
        levels = tally[:rows, at(c)]
        put("edge_levels", c, levels)
        spill = levels + lanes_to(levels, got("edge_levels", c - 1, rows), 1)
        put("edge_spill", c, spill)
        yield
        spill2 = lanes_to(spill, got("edge_spill", c - 1, rows), 2)
        power_e, power_s = jnp.exp2(log_e), jnp.exp2(log_s)
        flux_e = edge[2, :, at(c)] * FLOW
        flux_s = jnp.concatenate([raw[3, inner:, at(c)], edge[3, :, at(c)]], axis=0) * FLOW
        yield
        damp_e = damping(flux_e, drag, power_e)
        damp_s = damping(flux_s, drag_b, power_s)
        yield
        new_east = closed_east(c, (flux_e - depth_e * (east - here)) * damp_e)
        new_south = closed_south((flux_s - depth_s * (below_s - whole[inner:])) * damp_s)
        fe[outer, at(c)] = new_east
        fs[inner:, at(c)] = new_south
        bottoms[0, :, at(c)] = new_south[:TILE]
        put("edge_east", c, new_east)
        west = lanes_to(new_east, got("edge_east", c - 1, TILE), 1)
        new_south = jnp.concatenate([fs[:inner, at(c)], new_south], axis=0)
        yield
        gain_s = north(new_south) - new_south
        surf[:rows, at(c)] = (
            partial[:, at(c)]
            + gain_s[:rows]
            + (spill + spill2 - number4[:rows, at(c)] * whole[:rows])
        )
        surf[outer, at(c)] = here + (west - new_east) + gain_s[rows:]

    def edge_source(c):
        spill = spilled("edge_moved", c, tally[outer, at(c)])
        yield
        source = spill()
        yield
        here = (edge[0, :, at(c)] + edge[1, :, at(c)]) * LEVEL
        surf[outer, at(c)] = surf[outer, at(c)] + (source - number4[outer, at(c)] * here)

    def spilled(name, c, moved):
        count = moved.shape[0]
        put((name, 1), c, moved)
        once = moved + lanes_to(moved, got((name, 1), c - 1, count), 1)
        put((name, 2), c, once)
        return lambda: once + lanes_to(once, got((name, 2), c - 1, count), 2)

    def halo_step(step, c):
        if step == 0:
            floor = edge[1, :, at(c)] * LEVEL
            here = edge[0, :, at(c)] * LEVEL + floor
            mine = roughness(edge_rough[:, at(c)])
            turned = [turn(a, 1) for a in (here, floor, mine)]
        else:
            here = surf[outer, at(c)]
            turned = [turn(here, 1)]
        put(("halo", step), c, turned)
        yield
        yield
        following = after.get((("halo", step), c + 1), [zeros(TILE)] * 3)
        nexts = [jnp.where(lane_id < LANES - 1, a, b) for a, b in zip(turned, following)]
        east = nexts[0]
        pair = here + east
        put(("halo_pair", step), c, turn(pair, 2))

        def southward(value, top):
            return south(jnp.concatenate([value, top], axis=0))[:TILE]

        below_s = southward(here, tops[step, :, at(c)])
        if step == 0:
            top = jnp.maximum(floor, nexts[1])
            drag = square(mine + nexts[2])
            top_s = jnp.maximum(floor, southward(floor, bed[:TILE, at(c)]))
            drag_b = square(mine + southward(mine, mann[:TILE, at(c)]))
            max_e[outer, at(c)] = top
            drag_e[outer, at(c)] = drag
            max_s[outer, at(c)] = top_s
            drag_s[outer, at(c)] = drag_b
            flux_e, flux_s = (edge[i, :, at(c)] * FLOW for i in (2, 3))
            moved = tally[outer, at(c)]
        else:
            top, drag = max_e[outer, at(c)], drag_e[outer, at(c)]
            top_s, drag_b = max_s[outer, at(c)], drag_s[outer, at(c)]
            flux_e, flux_s = fe[outer, at(c)], fs[outer, at(c)]
            box = boxes[outer, at(c)]
            moved = number[outer, at(c)] * box + KEEP**step * tally[outer, at(c)]
        depth_e = depth_of(here, east, top)
        log_e = power_log(depth_e)
        depth_s = depth_of(here, below_s, top_s)
        log_s = power_log(depth_s)
        spill = spilled(("halo_moved", step), c, moved)
        yield
        power_e, power_s = jnp.exp2(log_e), jnp.exp2(log_s)
        source = spill()
        yield
        total = pair + two_on(("halo_pair", step), c, TILE)
        boxes[outer, at(c)] = total if step == 0 else KEEP * box + total
        damp_e = damping(flux_e, drag, power_e)
        damp_s = damping(flux_s, drag_b, power_s)
        source = source - number4[outer, at(c)] * here
        yield
        new_east = closed_east(c, (flux_e - depth_e * (east - here)) * damp_e)
        new_south = (flux_s - depth_s * (below_s - here)) * damp_s
        new_south = jnp.where(shut_first, 0.0, new_south)
        put(("halo_east", step), c, new_east)
        west = lanes_to(new_east, got(("halo_east", step), c - 1, TILE), 1)
        fe[outer, at(c)] = new_east
        fs[outer, at(c)] = new_south
        yield
        into = north(jnp.concatenate([bottoms[step, :, at(c)], new_south], axis=0))[TILE:]
        surf[outer, at(c)] = here + (west - new_east) + (into - new_south) + source

    def part_chunk(step, c):
        last = step == STEPS - 1
        here = surf[:rows, at(c)]
        turned = turn(here, 1)
        put(("here", step), c, (here, turned))
        if not last:
            tops[step, :, at(c)] = here[:TILE]
        yield
        yield
        following = after.get((("here", step), c + 1), (zeros(rows), zeros(rows)))
        east = jnp.where(lane_id < LANES - 1, turned, following[1])
        depth_e = depth_of(here, east, max_e[:rows, at(c)])
        log_e = power_log(depth_e)
        below_s = south(here)[:inner]
        depth_s = depth_of(here[:inner], below_s, max_s[:inner, at(c)])
        log_s = power_log(depth_s)
        if not last:
            pair = here + east
            put(("pair", step), c, turn(pair, 2))
        box = boxes[:rows, at(c)]
        spill = spilled(
            ("moved", step), c, number[:rows, at(c)] * box + KEEP**step * tally[:rows, at(c)]
        )
        yield
        power_e, power_s = jnp.exp2(log_e), jnp.exp2(log_s)
        source = spill()
        yield
        if not last:
            boxes[:rows, at(c)] = KEEP * box + (pair + two_on(("pair", step), c, rows))
        flux_e, flux_s = fe[:rows, at(c)], fs[:inner, at(c)]
        damp_e = damping(flux_e, drag_e[:rows, at(c)], power_e)
        damp_s = damping(flux_s, drag_s[:inner, at(c)], power_s)
        source = source - number4[:rows, at(c)] * here
        yield
        new_east = closed_east(c, (flux_e - depth_e * (east - here)) * damp_e)
        new_south = (flux_s - depth_s * (below_s - here[:inner])) * damp_s
        put(("east", step), c, new_east)
        west = lanes_to(new_east, got(("east", step), c - 1, rows), 1)
        fs[:inner, at(c)] = new_south
        if last:
            east_out[:, at(c)] = new_east * (1.0 / FLOW)
            south_out[:inner, at(c)] = new_south * (1.0 / FLOW)
        else:
            fe[:rows, at(c)] = new_east
        yield
        partial[:, at(c)] = here + (west - new_east) + source

    def join_chunk(step, c):
        last = step == STEPS - 1
        whole = jnp.concatenate([surf[inner:, at(c)], surf[:TILE, at(c)]], axis=0)
        here = whole[: 2 * TILE]
        below_s = south(whole)[: 2 * TILE]
        depth_s = depth_of(here, below_s, max_s[inner:, at(c)])
        log_s = power_log(depth_s)
        yield
        power_s = jnp.exp2(log_s)
        flux_s = fs[inner:, at(c)]
        yield
        damp_s = damping(flux_s, drag_s[inner:, at(c)], power_s)
        yield
        new_south = closed_south((flux_s - depth_s * (below_s - here)) * damp_s)
        if last:
            south_out[inner:, at(c)] = new_south[:TILE] * (1.0 / FLOW)
        else:
            fs[inner:rows, at(c)] = new_south[:TILE]
            bottoms[step, :, at(c)] = new_south[:TILE]
        new_south = jnp.concatenate([fs[:inner, at(c)], new_south], axis=0)
        level = partial[:, at(c)] + (north(new_south) - new_south)[:rows]
        if last:
            depth_out[:, at(c)] = level * (1.0 / LEVEL) - raw[1, :, at(c)]
        else:
            surf[:rows, at(c)] = level

    def arrive(tier):
        for offset in (-1, 1):
            @pl.when(there(-offset))
            def _():
                for copy in strip_sends[tier, offset]:
                    copy.wait_recv()

                for j in range(4):
                    lands = landing(tier, j, offset)
                    edge[j, lands, :] = far[tier - 1, j, lands, :]
                lands = landing(tier, 4, offset)
                edge_rough[lands, :] = far_rough[tier - 1, lands, :]

    def again(steps, step, extra):
        batches = []
        for done in range(steps):
            batches += by(5, (halo_step(done, c) for c in range(chunks))) + [[]] * 4
        for i, batch in enumerate(by(5, (part_chunk(step, c) for c in range(chunks)))):
            batches[i + 3] = batches[i + 3] + batch
        wave(batches + by(5, (join_chunk(step, c) for c in range(chunks))) + extra)

    flat = {}

    def node_chunk(c):
        here = surf[:rows, at(c)]
        turned = turn(here, 1)
        put("node", c, (here, turned))
        yield
        yield
        following = after.get(("node", c + 1), (zeros(rows), zeros(rows)))
        pair = here + jnp.where(lane_id < LANES - 1, turned, following[1])
        put("node_pair", c, turn(pair, 2))
        yield
        yield
        flat[c] = KEEP * boxes[:rows, at(c)] + (pair + two_on("node_pair", c, rows))

    wave(
        by(15, (edge_chunk(c) for c in range(chunks)))
        + [[]] * 5
        + by(5, (part_chunk(1, c) for c in range(chunks)))
    )

    nodes_of((-2, 2))
    _, _, _, place_f, _, weights_f = locate((0, 4))
    spread = spread_by(one_hot(blocks, place_f), weights_f)
    for c in range(chunks):
        level, count = planes(spread[c * TILE : (c + 1) * TILE])
        level = level + tally[outer, at(c)]
        share("edge", outer, c, level, count + number[outer, at(c)])
    wave(
        by(15, (edge_source(c) for c in range(chunks)))
        + [[]]
        + by(5, (join_chunk(1, c) for c in range(chunks)))
    )

    arrive(1)
    again(2, 2, by(5, (node_chunk(c) for c in range(chunks))))
    flat = [flat[c] for c in range(chunks)]

    turned = jnp.concatenate(halves(jnp.concatenate(flat, axis=0).T), axis=0)

    def levels_of(section, own, hit, lane_hit):
        picked = jnp.dot(turned, hit, preferred_element_type=jnp.float32)
        picked = picked[:LANES] + picked[LANES:]
        picked = jnp.sum(jnp.where(lane_hit, picked, 0.0), axis=0, keepdims=True)
        return jnp.where(own, KEEP**STEPS * section + (GAIN / LEVEL) * picked, 0.0)

    final = levels_of(section_n, own_n, hit_n, lane_n)
    part[0] = final[:, :owned]
    part[2] = final[:, owned:]

    part_prev = send(part.at[0], high, part_ssem.at[0], part_rsem.at[0], -1)
    part_next = send(part.at[2], low, part_ssem.at[1], part_rsem.at[1], 1)

    @pl.when(there(-1))
    def _():
        part_prev.start()

    @pl.when(there(1))
    def _():
        part_next.start()

    part[1] = levels_of(section_m, own_m, hit_m, lane_m)

    arrive(2)
    again(3, 3, [])

    for offset in OFFSETS:
        @pl.when(there(offset))
        def _():
            for copy in node_sends[offset]:
                copy.wait_send()

    for offset in (-1, 1):
        @pl.when(there(offset))
        def _():
            for tier in range(len(TIERS)):
                for copy in strip_sends[tier, offset]:
                    copy.wait_send()

    section_out[...] = part[1]

    @pl.when(there(1))
    def _():
        part_prev.wait_recv()
        section_out[...] += high[...]

    @pl.when(there(-1))
    def _():
        part_next.wait_recv()
        section_out[...] += low[...]

    @pl.when(there(-1))
    def _():
        part_prev.wait_send()

    @pl.when(there(1))
    def _():
        part_next.wait_send()


def finish_kernel(a, b, c, d, a_out, b_out, c_out, d_out, out_sem):
    stores = [
        pltpu.make_async_copy(source, target, out_sem.at[i])
        for i, (source, target) in enumerate(
            ((a, a_out), (b, b_out), (c, c_out), (d, d_out))
        )
    ]
    for store in stores:
        store.start()
    for store in stores:
        store.wait()


def finish(*arrays):
    return pl.pallas_call(
        finish_kernel,
        out_shape=[jax.ShapeDtypeStruct(a.shape, a.dtype) for a in arrays],
        in_specs=[pl.BlockSpec(memory_space=pltpu.VMEM)] * 4,
        out_specs=[pl.BlockSpec(memory_space=pltpu.MemorySpace.HBM)] * 4,
        scratch_shapes=[pltpu.SemaphoreType.DMA((4,))],
        compiler_params=pltpu.CompilerParams(vmem_limit_bytes=VMEM_BYTES),
        name="finish",
    )(*arrays)


def local(
    depth, flux_east, flux_south, river_section, bed_level, rough_class, manning_table, bank_cell
):
    rows, columns = depth.shape
    owned = river_section.shape[0]
    width, _ = bank_cell.shape
    ext = rows + 2 * HALO
    operands = [
        pltpu.with_memory_space_constraint(a, pltpu.MemorySpace.HBM)
        for a in (
            manning_table,
            depth,
            flux_east,
            flux_south,
            bed_level,
            rough_class,
            river_section.reshape(1, owned),
            bank_cell,
        )
    ]
    hbm = pl.BlockSpec(memory_space=pltpu.MemorySpace.HBM)
    vmem = pl.BlockSpec(memory_space=pltpu.VMEM)
    tile = pltpu.VMEM((rows, columns), jnp.float32)
    line = pltpu.VMEM((1, owned), jnp.float32)
    wide = pltpu.VMEM((ext, columns), jnp.float32)
    dma = pltpu.SemaphoreType.DMA
    depth, flux_east, flux_south, section = pl.pallas_call(
        flood_kernel,
        out_shape=[tile, tile, tile, line],
        in_specs=[hbm] * 8,
        out_specs=[vmem] * 4,
        scratch_shapes=[
            pltpu.SMEM(manning_table.shape, jnp.float32),
            pltpu.VMEM((4, rows, columns), jnp.float32),
            pltpu.VMEM((rows, columns), jnp.int32),
            pltpu.VMEM((4, 2 * HALO, columns), jnp.float32),
            pltpu.VMEM((2 * HALO, columns), jnp.int32),
            pltpu.VMEM((len(TIERS) - 1, 4, 2 * HALO, columns), jnp.float32),
            pltpu.VMEM((len(TIERS) - 1, 2 * HALO, columns), jnp.int32),
            pltpu.VMEM((STEPS - 1, TILE, columns), jnp.float32),
            pltpu.VMEM((STEPS - 1, TILE, columns), jnp.float32),
        ]
        + [wide] * 13
        + [
            tile,
            pltpu.VMEM((5, 1, owned), jnp.float32),
            pltpu.VMEM((5, width, owned), jnp.int32),
            pltpu.VMEM((3, 1, owned), jnp.float32),
            line,
            line,
            dma((8,)),
            dma((2, 15)),
            dma((2, 15)),
            dma((2, 4)),
            dma((2, 4)),
            dma((2,)),
            dma((2,)),
        ],
        compiler_params=pltpu.CompilerParams(
            collective_id=0, has_side_effects=True, vmem_limit_bytes=VMEM_BYTES
        ),
        name="flood",
    )(*operands)
    depth, flux_east, flux_south, section = finish(depth, flux_east, flux_south, section)
    return depth, flux_east, flux_south, section.reshape(owned)


def solution(mesh):
    return jax.shard_map(
        local,
        mesh=mesh,
        in_specs=(
            P(("runs", "gy"), None),
            P(("runs", "gy"), None),
            P(("runs", "gy"), None),
            P(("runs", "gy")),
            P("gy", None),
            P("gy", None),
            P(),
            P(None, "gy"),
        ),
        out_specs=(
            P(("runs", "gy"), None),
            P(("runs", "gy"), None),
            P(("runs", "gy"), None),
            P(("runs", "gy")),
        ),
        check_vma=False,
    )
```

```python
import math

import jax
import jax.numpy as jnp
from jax import lax
from jax.experimental import pallas as pl
from jax.experimental.pallas import tpu as pltpu
from jax.sharding import PartitionSpec as P

STEPS = 4
HALO = STEPS
TIERS = ((0, 2), (2, 3), (3, 4))
LANES = 128
TILE = 8

GRAV = 9.81
TSTEP = 8.0
CELL = 90.0
FLOOR = 0.05
BANK_COEF = 200.0
CELL_AREA = 8100.0
NODE_AREA = 20000.0

SLOPE = GRAV * TSTEP / CELL
LEVEL = SLOPE * TSTEP / CELL
FLOW = LEVEL * TSTEP / CELL
ROUGH = math.sqrt(0.25 * GRAV * TSTEP * LEVEL ** (7.0 / 3.0) / FLOW)
KEEP = 1.0 - TSTEP * BANK_COEF * 4.0 / NODE_AREA
GAIN = TSTEP * BANK_COEF / NODE_AREA
INTO = TSTEP * BANK_COEF / CELL_AREA

MESH = pl.DeviceIdType.MESH
VMEM_BYTES = 24 * 1024 * 1024
FAR = -(1 << 24)
OFFSETS = (-1, 1, -2, 2)


def wave(batches):
    running, waiting = [], list(batches)
    while running or waiting:
        if waiting:
            running.extend(waiting.pop(0))
        for unit in list(running):
            try:
                next(unit)
            except StopIteration:
                running.remove(unit)


def by(size, units):
    units = list(units)
    return [units[i : i + size] for i in range(0, len(units), size)]


def halves(value):
    high = value.astype(jnp.bfloat16)
    return high, (value - high.astype(jnp.float32)).astype(jnp.bfloat16)


def flood_kernel(
    table_in,
    depth_in,
    east_in,
    south_in,
    bed_in,
    rough_in,
    section_in,
    cells_in,
    depth_out,
    east_out,
    south_out,
    section_out,
    table,
    raw,
    raw_rough,
    edge,
    edge_rough,
    far,
    far_rough,
    tops,
    bottoms,
    surf,
    fe,
    fs,
    bed,
    mann,
    max_e,
    max_s,
    drag_e,
    drag_s,
    tally,
    number,
    number4,
    boxes,
    partial,
    sections,
    cells,
    part,
    low,
    high,
    in_sem,
    strip_ssem,
    strip_rsem,
    node_ssem,
    node_rsem,
    part_ssem,
    part_rsem,
):
    me = lax.axis_index("gy")
    tiles = lax.axis_size("gy")
    rows, columns = depth_in.shape
    ext = rows + 2 * HALO
    chunks = columns // LANES
    owned = section_in.shape[1]
    total = 5 * owned

    def there(offset):
        return (me + offset >= 0) & (me + offset < tiles)

    def absent(offset):
        return jnp.logical_not(there(offset))

    edge[...] = jnp.zeros(edge.shape, jnp.float32)
    edge_rough[...] = jnp.zeros(edge_rough.shape, jnp.int32)
    barrier = pltpu.get_barrier_semaphore()
    for offset in OFFSETS:
        @pl.when(there(offset))
        def _():
            pl.semaphore_signal(
                barrier, inc=1, device_id={"gy": me + offset}, device_id_type=MESH
            )

    fields = (depth_in, bed_in, east_in, south_in)
    loads = [
        pltpu.make_async_copy(source, target, in_sem.at[i])
        for i, (source, target) in enumerate(
            [(field, raw.at[i]) for i, field in enumerate(fields)]
            + [
                (rough_in, raw_rough),
                (table_in, table),
                (section_in, sections.at[2]),
                (cells_in, cells.at[2]),
            ]
        )
    ]
    for load in loads:
        load.start()

    def send(src, dst, ssem, rsem, offset):
        return pltpu.make_async_remote_copy(
            src_ref=src,
            dst_ref=dst,
            send_sem=ssem,
            recv_sem=rsem,
            device_id={"gy": me + offset},
            device_id_type=MESH,
        )

    node_sends = {}
    for i, offset in enumerate(OFFSETS):
        slot = 2 - offset
        node_sends[offset] = (
            send(section_in, sections.at[slot], node_ssem.at[0, i], node_rsem.at[0, i], offset),
            send(cells_in, cells.at[slot], node_ssem.at[1, i], node_rsem.at[1, i], offset),
        )
    def span_of(tier, field, offset):
        first, stop = TIERS[tier]
        if field == 2 or (field == 3 and offset < 0):
            return max(first - 1, 0), stop - 1
        return first, stop

    def landing(tier, field, offset):
        first, stop = span_of(tier, field, offset)
        return slice(first, stop) if offset < 0 else slice(2 * HALO - stop, 2 * HALO - first)

    strip_sends = {}
    for i, offset in enumerate((-1, 1)):
        for tier in range(len(TIERS)):
            strip_sends[tier, offset] = []
            for j in range(5):
                first, stop = span_of(tier, j, offset)
                theirs = slice(first, stop) if offset < 0 else slice(rows - stop, rows - first)
                lands = landing(tier, j, offset)
                if j < 4:
                    source = fields[j].at[theirs]
                    target = edge.at[j, lands] if tier == 0 else far.at[tier - 1, j, lands]
                else:
                    source = rough_in.at[theirs]
                    target = edge_rough.at[lands] if tier == 0 else far_rough.at[tier - 1, lands]
                sem = 5 * tier + j
                strip_sends[tier, offset].append(
                    send(source, target, strip_ssem.at[i, sem], strip_rsem.at[i, sem], offset)
                )

    pl.semaphore_wait(barrier, jnp.minimum(me, 2) + jnp.minimum(tiles - 1 - me, 2))
    for offset in OFFSETS:
        @pl.when(there(offset))
        def _():
            for copy in node_sends[offset]:
                copy.start()

    def launch(*tiers_now):
        for offset in (-1, 1):
            @pl.when(there(offset))
            def _():
                for tier in tiers_now:
                    for copy in strip_sends[tier, offset]:
                        copy.start()

    launch(0)

    for load in loads:
        load.wait()

    scaled = [table[k] * ROUGH for k in range(table.shape[0])]

    def roughness(rough):
        values, bit = scaled, 1
        while len(values) > 1:
            odd = (rough & bit) != 0
            values = [
                jnp.where(odd, values[i + 1], values[i]) if i + 1 < len(values) else values[i]
                for i in range(0, len(values), 2)
            ]
            bit *= 2
        return values[0]

    def at(c):
        return slice(LANES * c, LANES * (c + 1))

    lane_id = lax.broadcasted_iota(jnp.int32, (1, LANES), 1)

    def turn(value, shift):
        return pltpu.roll(value, LANES - shift, 1)

    def lanes_to(value, preceding, shift):
        mixed = jnp.where(lane_id < LANES - shift, value, preceding)
        return pltpu.roll(mixed, shift, 1)

    def south(value):
        return pltpu.roll(value, value.shape[0] - 1, 0)

    def north(value):
        return pltpu.roll(value, 1, 0)

    row_id = lax.broadcasted_iota(jnp.int32, (TILE, LANES), 0)
    shut_last = (row_id == TILE - 1) & (me == tiles - 1)
    shut_first = (row_id == TILE - 1) & (me == 0)

    def depth_of(surf_a, surf_b, bed_top):
        return jnp.maximum(jnp.maximum(surf_a, surf_b) - bed_top, FLOOR * LEVEL)

    def power_log(flow_depth):
        return lax.log2(flow_depth) * (-7.0 / 3.0)

    def damping(flux, drag, power):
        return 1.0 / (1.0 + drag * jnp.abs(flux) * power)

    def square(value):
        return value * value

    def closed_east(c, flux):
        return jnp.where(lane_id == LANES - 1, 0.0, flux) if c == chunks - 1 else flux

    def closed_south(flux):
        count = flux.shape[0]
        return jnp.concatenate(
            [flux[: count - 2 * TILE]] * (count > 2 * TILE)
            + [
                jnp.where(shut_last, 0.0, flux[count - 2 * TILE : count - TILE]),
                jnp.where(shut_first, 0.0, flux[count - TILE :]),
            ],
            axis=0,
        )

    def last_four(value, carried):
        pair = value + lanes_to(value, carried[0], 1)
        return pair + lanes_to(pair, carried[1], 2), (value, pair)

    def zeros(count):
        return jnp.zeros((count, LANES), jnp.float32)

    after = {}

    def put(name, c, value):
        after[name, c] = value

    def got(name, c, count):
        return after.get((name, c), zeros(count))

    def two_on(name, c, count):
        return jnp.where(lane_id < LANES - 2, after[name, c], got(name, c + 1, count))

    inner = rows - TILE

    def own_chunk(c):
        floor = raw[1, :, at(c)] * LEVEL
        bed[:rows, at(c)] = floor
        mine = roughness(raw_rough[:, at(c)])
        mann[:rows, at(c)] = mine
        here = raw[0, :, at(c)] * LEVEL + floor
        surf[:rows, at(c)] = here
        tops[0, :, at(c)] = here[:TILE]
        turned = [turn(a, 1) for a in (here, floor, mine)]
        put("own", c, (here, turned))
        yield
        yield
        following = after.get(("own", c + 1), (zeros(rows), [zeros(rows)] * 3))
        east, floor_e, mann_e = (
            jnp.where(lane_id < LANES - 1, a, b) for a, b in zip(turned, following[1])
        )
        pair = here + east
        put("pair", c, turn(pair, 2))
        top = jnp.maximum(floor, floor_e)
        drag = square(mine + mann_e)
        max_e[:rows, at(c)] = top
        drag_e[:rows, at(c)] = drag
        depth_e = depth_of(here, east, top)
        log_e = power_log(depth_e)
        below_s = south(here)[:inner]
        top = jnp.maximum(floor, south(floor))[:inner]
        drag_b = square((mine + south(mine))[:inner])
        max_s[:inner, at(c)] = top
        drag_s[:inner, at(c)] = drag_b
        depth_s = depth_of(here[:inner], below_s, top)
        log_s = power_log(depth_s)
        yield
        power_e, power_s = jnp.exp2(log_e), jnp.exp2(log_s)
        flux_e = raw[2, :, at(c)] * FLOW
        flux_s = raw[3, :inner, at(c)] * FLOW
        yield
        boxes[:rows, at(c)] = pair + two_on("pair", c, rows)
        damp_e = damping(flux_e, drag, power_e)
        damp_s = damping(flux_s, drag_b, power_s)
        yield
        new_east = closed_east(c, (flux_e - depth_e * (east - here)) * damp_e)
        new_south = (flux_s - depth_s * (below_s - here[:inner])) * damp_s
        fe[:rows, at(c)] = new_east
        fs[:inner, at(c)] = new_south
        put("east", c, new_east)
        west = lanes_to(new_east, got("east", c - 1, rows), 1)
        yield
        partial[:, at(c)] = here + (west - new_east)

    wave(by(2, (own_chunk(c) for c in range(chunks))))
    after.clear()

    launch(1, 2)

    def nodes_of(offsets):
        for offset in offsets:
            @pl.when(there(-offset))
            def _():
                for copy in node_sends[offset]:
                    copy.wait_recv()

            @pl.when(absent(-offset))
            def _():
                sections[2 - offset] = jnp.zeros((1, owned), jnp.float32)
                cells[2 - offset] = jnp.full((cells.shape[1], owned), FAR, jnp.int32)

    def one_hot(count, index):
        found = lax.broadcasted_iota(jnp.int32, (count, index.shape[1]), 0) == index
        return jnp.where(found, 1.0, 0.0).astype(jnp.bfloat16)

    def locate(slots):
        section = jnp.concatenate([sections[i] for i in slots], axis=1)
        cell = jnp.concatenate([cells[i, 0:1, :] for i in slots], axis=1)
        local = cell - (me * rows - HALO) * columns
        valid = (local >= 0) & (local < ext * columns)
        local = jnp.where(valid, local, 0)
        from_top = ((local.astype(jnp.float32) + 0.5) * (1.0 / columns)).astype(jnp.int32)
        column = local - from_top * columns
        chunk = column >> 7
        own = valid & (from_top >= HALO) & (from_top < rows + HALO)
        place = jnp.where(own, chunk * rows + from_top - HALO, -1)
        beyond = jnp.where(from_top < HALO, from_top + HALO, from_top - rows - HALO)
        place_edge = jnp.where(valid & jnp.logical_not(own), chunk * TILE + beyond, -1)
        lane = column & (LANES - 1)
        lane_hit = lax.broadcasted_iota(jnp.int32, (LANES, lane.shape[1]), 0) == lane
        levels = section * (LEVEL * INTO)
        level_high = levels.astype(jnp.bfloat16).astype(jnp.float32)
        weights = jnp.concatenate(
            [
                jnp.where(lane_hit, value, 0.0)
                for value in (level_high, levels - level_high, jnp.ones_like(levels))
            ],
            axis=0,
        ).astype(jnp.bfloat16)
        return section, own, place, place_edge, lane_hit, weights

    def spread_by(hits, weights):
        return lax.dot_general(
            hits, weights, (((1,), (1,)), ((), ())), preferred_element_type=jnp.float32
        )

    def planes(block):
        level = block[:, :LANES] + block[:, LANES : 2 * LANES]
        return level, block[:, 2 * LANES :] * INTO

    def share(name, span, c, level, count):
        count4, counted[name] = last_four(count, counted[name])
        tally[span, at(c)] = level
        number[span, at(c)] = count * GAIN
        number4[span, at(c)] = count4

    outer = slice(rows, ext)
    counted = {"own": (zeros(rows),) * 2, "edge": (zeros(TILE),) * 2}
    section_m, own_m, place, place_m, lane_m, weights_m = locate((2,))
    hit_m = one_hot(chunks * rows, place)
    spread = spread_by(hit_m, weights_m)
    for c in range(chunks):
        level, count = planes(spread[c * rows : (c + 1) * rows])
        tally[:rows, at(c)] = level
        number[:rows, at(c)] = count
    nodes_of((-1, 1))
    section_n, own_n, place, place_n, lane_n, weights_n = locate((1, 3))
    hit_n = one_hot(chunks * rows, place)
    spread = spread_by(hit_n, weights_n)
    for c in range(chunks):
        level, count = planes(spread[c * rows : (c + 1) * rows])
        level = level + tally[:rows, at(c)]
        share("own", slice(0, rows), c, level, count + number[:rows, at(c)])

    blocks = -(-chunks * TILE // 16) * 16
    spread = spread_by(
        one_hot(blocks, jnp.concatenate([place_m, place_n], axis=1)),
        jnp.concatenate([weights_m, weights_n], axis=1),
    )
    for c in range(chunks):
        level, count = planes(spread[c * TILE : (c + 1) * TILE])
        tally[outer, at(c)] = level
        number[outer, at(c)] = count

    for offset in (-1, 1):
        @pl.when(there(-offset))
        def _():
            for copy in strip_sends[0, offset]:
                copy.wait_recv()

    def edge_chunk(c):
        floor = edge[1, :, at(c)] * LEVEL
        here = edge[0, :, at(c)] * LEVEL + floor
        mine = roughness(edge_rough[:, at(c)])
        turned = [turn(a, 1) for a in (here, floor, mine)]
        put("edge", c, (here, turned))
        yield
        yield
        following = after.get(("edge", c + 1), (zeros(TILE), [zeros(TILE)] * 3))
        east, floor_e, mann_e = (
            jnp.where(lane_id < LANES - 1, a, b) for a, b in zip(turned, following[1])
        )
        top = jnp.maximum(floor, floor_e)
        drag = square(mine + mann_e)
        max_e[outer, at(c)] = top
        drag_e[outer, at(c)] = drag
        depth_e = depth_of(here, east, top)
        log_e = power_log(depth_e)
        whole = jnp.concatenate([surf[:rows, at(c)], here], axis=0)
        below_s = south(whole)[inner:]
        floor = jnp.concatenate([bed[:rows, at(c)], floor], axis=0)
        mine = jnp.concatenate([mann[:rows, at(c)], mine], axis=0)
        top = jnp.maximum(floor, south(floor))[inner:]
        drag_b = square((mine + south(mine))[inner:])
        max_s[inner:, at(c)] = top
        drag_s[inner:, at(c)] = drag_b
        depth_s = depth_of(whole[inner:], below_s, top)
        log_s = power_log(depth_s)
        levels = tally[:rows, at(c)]
        put("edge_levels", c, levels)
        spill = levels + lanes_to(levels, got("edge_levels", c - 1, rows), 1)
        put("edge_spill", c, spill)
        yield
        spill2 = lanes_to(spill, got("edge_spill", c - 1, rows), 2)
        power_e, power_s = jnp.exp2(log_e), jnp.exp2(log_s)
        flux_e = edge[2, :, at(c)] * FLOW
        flux_s = jnp.concatenate([raw[3, inner:, at(c)], edge[3, :, at(c)]], axis=0) * FLOW
        yield
        damp_e = damping(flux_e, drag, power_e)
        damp_s = damping(flux_s, drag_b, power_s)
        yield
        new_east = closed_east(c, (flux_e - depth_e * (east - here)) * damp_e)
        new_south = closed_south((flux_s - depth_s * (below_s - whole[inner:])) * damp_s)
        fe[outer, at(c)] = new_east
        fs[inner:, at(c)] = new_south
        bottoms[0, :, at(c)] = new_south[:TILE]
        put("edge_east", c, new_east)
        west = lanes_to(new_east, got("edge_east", c - 1, TILE), 1)
        new_south = jnp.concatenate([fs[:inner, at(c)], new_south], axis=0)
        yield
        gain_s = north(new_south) - new_south
        surf[:rows, at(c)] = (
            partial[:, at(c)]
            + gain_s[:rows]
            + (spill + spill2 - number4[:rows, at(c)] * whole[:rows])
        )
        surf[outer, at(c)] = here + (west - new_east) + gain_s[rows:]

    def edge_source(c):
        spill = spilled("edge_moved", c, tally[outer, at(c)])
        yield
        source = spill()
        yield
        here = (edge[0, :, at(c)] + edge[1, :, at(c)]) * LEVEL
        surf[outer, at(c)] = surf[outer, at(c)] + (source - number4[outer, at(c)] * here)

    def spilled(name, c, moved):
        count = moved.shape[0]
        put((name, 1), c, moved)
        once = moved + lanes_to(moved, got((name, 1), c - 1, count), 1)
        put((name, 2), c, once)
        return lambda: once + lanes_to(once, got((name, 2), c - 1, count), 2)

    def halo_step(step, c):
        if step == 0:
            floor = edge[1, :, at(c)] * LEVEL
            here = edge[0, :, at(c)] * LEVEL + floor
            mine = roughness(edge_rough[:, at(c)])
            turned = [turn(a, 1) for a in (here, floor, mine)]
        else:
            here = surf[outer, at(c)]
            turned = [turn(here, 1)]
        put(("halo", step), c, turned)
        yield
        yield
        following = after.get((("halo", step), c + 1), [zeros(TILE)] * 3)
        nexts = [jnp.where(lane_id < LANES - 1, a, b) for a, b in zip(turned, following)]
        east = nexts[0]
        pair = here + east
        put(("halo_pair", step), c, turn(pair, 2))

        def southward(value, top):
            return south(jnp.concatenate([value, top], axis=0))[:TILE]

        below_s = southward(here, tops[step, :, at(c)])
        if step == 0:
            top = jnp.maximum(floor, nexts[1])
            drag = square(mine + nexts[2])
            top_s = jnp.maximum(floor, southward(floor, bed[:TILE, at(c)]))
            drag_b = square(mine + southward(mine, mann[:TILE, at(c)]))
            max_e[outer, at(c)] = top
            drag_e[outer, at(c)] = drag
            max_s[outer, at(c)] = top_s
            drag_s[outer, at(c)] = drag_b
            flux_e, flux_s = (edge[i, :, at(c)] * FLOW for i in (2, 3))
            moved = tally[outer, at(c)]
        else:
            top, drag = max_e[outer, at(c)], drag_e[outer, at(c)]
            top_s, drag_b = max_s[outer, at(c)], drag_s[outer, at(c)]
            flux_e, flux_s = fe[outer, at(c)], fs[outer, at(c)]
            box = boxes[outer, at(c)]
            moved = number[outer, at(c)] * box + KEEP**step * tally[outer, at(c)]
        depth_e = depth_of(here, east, top)
        log_e = power_log(depth_e)
        depth_s = depth_of(here, below_s, top_s)
        log_s = power_log(depth_s)
        spill = spilled(("halo_moved", step), c, moved)
        yield
        power_e, power_s = jnp.exp2(log_e), jnp.exp2(log_s)
        source = spill()
        yield
        total = pair + two_on(("halo_pair", step), c, TILE)
        boxes[outer, at(c)] = total if step == 0 else KEEP * box + total
        damp_e = damping(flux_e, drag, power_e)
        damp_s = damping(flux_s, drag_b, power_s)
        source = source - number4[outer, at(c)] * here
        yield
        new_east = closed_east(c, (flux_e - depth_e * (east - here)) * damp_e)
        new_south = (flux_s - depth_s * (below_s - here)) * damp_s
        new_south = jnp.where(shut_first, 0.0, new_south)
        put(("halo_east", step), c, new_east)
        west = lanes_to(new_east, got(("halo_east", step), c - 1, TILE), 1)
        fe[outer, at(c)] = new_east
        fs[outer, at(c)] = new_south
        yield
        into = north(jnp.concatenate([bottoms[step, :, at(c)], new_south], axis=0))[TILE:]
        surf[outer, at(c)] = here + (west - new_east) + (into - new_south) + source

    def part_chunk(step, c):
        last = step == STEPS - 1
        here = surf[:rows, at(c)]
        turned = turn(here, 1)
        put(("here", step), c, (here, turned))
        if not last:
            tops[step, :, at(c)] = here[:TILE]
        yield
        yield
        following = after.get((("here", step), c + 1), (zeros(rows), zeros(rows)))
        east = jnp.where(lane_id < LANES - 1, turned, following[1])
        depth_e = depth_of(here, east, max_e[:rows, at(c)])
        log_e = power_log(depth_e)
        below_s = south(here)[:inner]
        depth_s = depth_of(here[:inner], below_s, max_s[:inner, at(c)])
        log_s = power_log(depth_s)
        if not last:
            pair = here + east
            put(("pair", step), c, turn(pair, 2))
        box = boxes[:rows, at(c)]
        spill = spilled(
            ("moved", step), c, number[:rows, at(c)] * box + KEEP**step * tally[:rows, at(c)]
        )
        yield
        power_e, power_s = jnp.exp2(log_e), jnp.exp2(log_s)
        source = spill()
        yield
        if not last:
            boxes[:rows, at(c)] = KEEP * box + (pair + two_on(("pair", step), c, rows))
        flux_e, flux_s = fe[:rows, at(c)], fs[:inner, at(c)]
        damp_e = damping(flux_e, drag_e[:rows, at(c)], power_e)
        damp_s = damping(flux_s, drag_s[:inner, at(c)], power_s)
        source = source - number4[:rows, at(c)] * here
        yield
        new_east = closed_east(c, (flux_e - depth_e * (east - here)) * damp_e)
        new_south = (flux_s - depth_s * (below_s - here[:inner])) * damp_s
        put(("east", step), c, new_east)
        west = lanes_to(new_east, got(("east", step), c - 1, rows), 1)
        fs[:inner, at(c)] = new_south
        if last:
            east_out[:, at(c)] = new_east * (1.0 / FLOW)
            south_out[:inner, at(c)] = new_south * (1.0 / FLOW)
        else:
            fe[:rows, at(c)] = new_east
        yield
        partial[:, at(c)] = here + (west - new_east) + source

    def join_chunk(step, c):
        last = step == STEPS - 1
        whole = jnp.concatenate([surf[inner:, at(c)], surf[:TILE, at(c)]], axis=0)
        here = whole[: 2 * TILE]
        below_s = south(whole)[: 2 * TILE]
        depth_s = depth_of(here, below_s, max_s[inner:, at(c)])
        log_s = power_log(depth_s)
        yield
        power_s = jnp.exp2(log_s)
        flux_s = fs[inner:, at(c)]
        yield
        damp_s = damping(flux_s, drag_s[inner:, at(c)], power_s)
        yield
        new_south = closed_south((flux_s - depth_s * (below_s - here)) * damp_s)
        if last:
            south_out[inner:, at(c)] = new_south[:TILE] * (1.0 / FLOW)
        else:
            fs[inner:rows, at(c)] = new_south[:TILE]
            bottoms[step, :, at(c)] = new_south[:TILE]
        new_south = jnp.concatenate([fs[:inner, at(c)], new_south], axis=0)
        level = partial[:, at(c)] + (north(new_south) - new_south)[:rows]
        if last:
            depth_out[:, at(c)] = level * (1.0 / LEVEL) - raw[1, :, at(c)]
        else:
            surf[:rows, at(c)] = level

    def arrive(tier):
        for offset in (-1, 1):
            @pl.when(there(-offset))
            def _():
                for copy in strip_sends[tier, offset]:
                    copy.wait_recv()

                for j in range(4):
                    lands = landing(tier, j, offset)
                    edge[j, lands, :] = far[tier - 1, j, lands, :]
                lands = landing(tier, 4, offset)
                edge_rough[lands, :] = far_rough[tier - 1, lands, :]

    def again(steps, step, extra):
        batches = []
        for done in range(steps):
            batches += by(5, (halo_step(done, c) for c in range(chunks))) + [[]] * 4
        for i, batch in enumerate(by(5, (part_chunk(step, c) for c in range(chunks)))):
            batches[i + 3] = batches[i + 3] + batch
        wave(batches + by(5, (join_chunk(step, c) for c in range(chunks))) + extra)

    flat = {}

    def node_chunk(c):
        here = surf[:rows, at(c)]
        turned = turn(here, 1)
        put("node", c, (here, turned))
        yield
        yield
        following = after.get(("node", c + 1), (zeros(rows), zeros(rows)))
        pair = here + jnp.where(lane_id < LANES - 1, turned, following[1])
        put("node_pair", c, turn(pair, 2))
        yield
        yield
        flat[c] = KEEP * boxes[:rows, at(c)] + (pair + two_on("node_pair", c, rows))

    wave(
        by(15, (edge_chunk(c) for c in range(chunks)))
        + [[]] * 5
        + by(5, (part_chunk(1, c) for c in range(chunks)))
    )

    nodes_of((-2, 2))
    _, _, _, place_f, _, weights_f = locate((0, 4))
    spread = spread_by(one_hot(blocks, place_f), weights_f)
    for c in range(chunks):
        level, count = planes(spread[c * TILE : (c + 1) * TILE])
        level = level + tally[outer, at(c)]
        share("edge", outer, c, level, count + number[outer, at(c)])
    wave(
        by(15, (edge_source(c) for c in range(chunks)))
        + [[]]
        + by(5, (join_chunk(1, c) for c in range(chunks)))
    )

    arrive(1)
    again(2, 2, by(5, (node_chunk(c) for c in range(chunks))))
    flat = [flat[c] for c in range(chunks)]

    turned = jnp.concatenate(halves(jnp.concatenate(flat, axis=0).T), axis=0)

    def levels_of(section, own, hit, lane_hit):
        picked = jnp.dot(turned, hit, preferred_element_type=jnp.float32)
        picked = picked[:LANES] + picked[LANES:]
        picked = jnp.sum(jnp.where(lane_hit, picked, 0.0), axis=0, keepdims=True)
        return jnp.where(own, KEEP**STEPS * section + (GAIN / LEVEL) * picked, 0.0)

    final = levels_of(section_n, own_n, hit_n, lane_n)
    part[0] = final[:, :owned]
    part[2] = final[:, owned:]

    part_prev = send(part.at[0], high, part_ssem.at[0], part_rsem.at[0], -1)
    part_next = send(part.at[2], low, part_ssem.at[1], part_rsem.at[1], 1)

    @pl.when(there(-1))
    def _():
        part_prev.start()

    @pl.when(there(1))
    def _():
        part_next.start()

    part[1] = levels_of(section_m, own_m, hit_m, lane_m)

    arrive(2)
    again(3, 3, [])

    for offset in OFFSETS:
        @pl.when(there(offset))
        def _():
            for copy in node_sends[offset]:
                copy.wait_send()

    for offset in (-1, 1):
        @pl.when(there(offset))
        def _():
            for tier in range(len(TIERS)):
                for copy in strip_sends[tier, offset]:
                    copy.wait_send()

    section_out[...] = part[1]

    @pl.when(there(1))
    def _():
        part_prev.wait_recv()
        section_out[...] += high[...]

    @pl.when(there(-1))
    def _():
        part_next.wait_recv()
        section_out[...] += low[...]

    @pl.when(there(-1))
    def _():
        part_prev.wait_send()

    @pl.when(there(1))
    def _():
        part_next.wait_send()


def finish_kernel(a, b, c, d, a_out, b_out, c_out, d_out, out_sem):
    stores = [
        pltpu.make_async_copy(source, target, out_sem.at[i])
        for i, (source, target) in enumerate(
            ((a, a_out), (b, b_out), (c, c_out), (d, d_out))
        )
    ]
    for store in stores:
        store.start()
    for store in stores:
        store.wait()


def finish(*arrays):
    return pl.pallas_call(
        finish_kernel,
        out_shape=[jax.ShapeDtypeStruct(a.shape, a.dtype) for a in arrays],
        in_specs=[pl.BlockSpec(memory_space=pltpu.VMEM)] * 4,
        out_specs=[pl.BlockSpec(memory_space=pltpu.MemorySpace.HBM)] * 4,
        scratch_shapes=[pltpu.SemaphoreType.DMA((4,))],
        compiler_params=pltpu.CompilerParams(vmem_limit_bytes=VMEM_BYTES),
        name="finish",
    )(*arrays)


def local(
    depth, flux_east, flux_south, river_section, bed_level, rough_class, manning_table, bank_cell
):
    rows, columns = depth.shape
    owned = river_section.shape[0]
    width, _ = bank_cell.shape
    ext = rows + 2 * HALO
    operands = [
        pltpu.with_memory_space_constraint(a, pltpu.MemorySpace.HBM)
        for a in (
            manning_table,
            depth,
            flux_east,
            flux_south,
            bed_level,
            rough_class,
            river_section.reshape(1, owned),
            bank_cell,
        )
    ]
    hbm = pl.BlockSpec(memory_space=pltpu.MemorySpace.HBM)
    vmem = pl.BlockSpec(memory_space=pltpu.VMEM)
    tile = pltpu.VMEM((rows, columns), jnp.float32)
    line = pltpu.VMEM((1, owned), jnp.float32)
    wide = pltpu.VMEM((ext, columns), jnp.float32)
    dma = pltpu.SemaphoreType.DMA
    depth, flux_east, flux_south, section = pl.pallas_call(
        flood_kernel,
        out_shape=[tile, tile, tile, line],
        in_specs=[hbm] * 8,
        out_specs=[vmem] * 4,
        scratch_shapes=[
            pltpu.SMEM(manning_table.shape, jnp.float32),
            pltpu.VMEM((4, rows, columns), jnp.float32),
            pltpu.VMEM((rows, columns), jnp.int32),
            pltpu.VMEM((4, 2 * HALO, columns), jnp.float32),
            pltpu.VMEM((2 * HALO, columns), jnp.int32),
            pltpu.VMEM((len(TIERS) - 1, 4, 2 * HALO, columns), jnp.float32),
            pltpu.VMEM((len(TIERS) - 1, 2 * HALO, columns), jnp.int32),
            pltpu.VMEM((STEPS - 1, TILE, columns), jnp.float32),
            pltpu.VMEM((STEPS - 1, TILE, columns), jnp.float32),
        ]
        + [wide] * 13
        + [
            tile,
            pltpu.VMEM((5, 1, owned), jnp.float32),
            pltpu.VMEM((5, width, owned), jnp.int32),
            pltpu.VMEM((3, 1, owned), jnp.float32),
            line,
            line,
            dma((8,)),
            dma((2, 15)),
            dma((2, 15)),
            dma((2, 4)),
            dma((2, 4)),
            dma((2,)),
            dma((2,)),
        ],
        compiler_params=pltpu.CompilerParams(
            collective_id=0, has_side_effects=True, vmem_limit_bytes=VMEM_BYTES
        ),
        name="flood",
    )(*operands)
    depth, flux_east, flux_south, section = finish(depth, flux_east, flux_south, section)
    return depth, flux_east, flux_south, section.reshape(owned)


def solution(mesh):
    return jax.shard_map(
        local,
        mesh=mesh,
        in_specs=(
            P(("runs", "gy"), None),
            P(("runs", "gy"), None),
            P(("runs", "gy"), None),
            P(("runs", "gy")),
            P("gy", None),
            P("gy", None),
            P(),
            P(None, "gy"),
        ),
        out_specs=(
            P(("runs", "gy"), None),
            P(("runs", "gy"), None),
            P(("runs", "gy"), None),
            P(("runs", "gy")),
        ),
        check_vma=False,
    )
```
